32 devices in a mesh: box: 16 (over z, y, x), col: 2 (over core).
Axes of the slice: x: 2, y: 2, z: 4, core: 2. Of those that a mesh axis runs over, the one named last changes fastest.
Arguments:
- points: bfloat16 [256, 3, 512], P('box'), may hold values from 0 to 1
- sketch: bfloat16 [256, 512, 128], P('box', 'col'), may hold values from -6 to 6
- near_mask: int32 [256, 9], P('box'), may hold values from 0 to 1, as said below
Outputs:
- basis: bfloat16 [256, 512, 128], P('box', 'col')
- coupling: float32 [256, 9, 128, 128], P('box', None, 'col')
The draws below stay inside these ranges and needn't reach their ends.
Inputs may be any that keep to these rules, and one draw needn't show every extreme that they name: near_mask[b, s] is 1 for the box itself and for its edge neighbours that lie on the plate, 0 for slots off the plate; a diagonal neighbour is near or not by a relation that is symmetric between the two boxes.
All inputs are finite; a program needn't handle non-finite values.
Results may differ from the reference program's by a relative error of at most 0.007.
Values may be sent and summed in bfloat16 or wider, within the bound.
No kernel may reach another device: no remote copies, remote signals or barrier semaphores. Data moves between devices by JAX's collectives and lax.ppermute only.
A program may use at most 64 MiB of HBM per device.

```python
import math
import jax
import jax.numpy as jnp
from jax import lax

M = 512
R = 128
TILE = 4
DGRID = 4
NB = 256


def draw_near_mask(key, part):
    plate_side = TILE * DGRID
    diag_down = jax.random.randint(jax.random.fold_in(key, 11), (plate_side, plate_side), 0, 2)
    diag_up = jax.random.randint(jax.random.fold_in(key, 12), (plate_side, plate_side), 0, 2)
    middle = plate_side // 2
    grid_rows = jnp.arange(plate_side)[:, None]
    grid_cols = jnp.arange(plate_side)[None, :]
    force_down = (grid_rows == middle) & (grid_cols == middle) | (grid_rows == middle - 1) & (grid_cols == middle - 1)
    force_up = (grid_rows == middle) & (grid_cols == middle - 1) | (grid_rows == middle - 1) & (grid_cols == middle)
    diag_down = jnp.where(force_down, 1, diag_down)
    diag_up = jnp.where(force_up, 1, diag_up)
    box_ids = jnp.arange(NB, dtype=jnp.int32)
    group_ids = box_ids // (TILE * TILE)
    local_ids = box_ids % (TILE * TILE)
    grid_y = group_ids // DGRID * TILE + local_ids // TILE
    grid_x = group_ids % DGRID * TILE + local_ids % TILE
    columns = []
    for stencil in range(9):
        offset_y = stencil // 3 - 1
        offset_x = stencil % 3 - 1
        near_y = grid_y + offset_y
        near_x = grid_x + offset_x
        inside = (near_y >= 0) & (near_y < plate_side) & (near_x >= 0) & (near_x < plate_side)
        if offset_y == 0 or offset_x == 0:
            allowed = inside
        else:
            low_y = jnp.clip(jnp.minimum(grid_y, near_y), 0, plate_side - 1)
            low_x = jnp.clip(jnp.minimum(grid_x, near_x), 0, plate_side - 1)
            bit_table = diag_down if offset_y == offset_x else diag_up
            allowed = inside & (bit_table[low_y, low_x] == 1)
        columns.append(allowed.astype(jnp.int32))
    return jnp.stack(columns, axis=1)


def shard_levels(own_key, shape, pieces, smallest, top_value):
    def one(dim, shards_of):
        steps = jax.random.uniform(jax.random.fold_in(jax.random.fold_in(own_key, 6), dim), (shards_of,), jnp.float32, smallest / len(pieces), top_value / len(pieces))
        return jnp.repeat(jnp.exp(steps), shape[dim] // shards_of).reshape((-1,) + (1,) * (len(shape) - dim - 1))

    loudness = one(*pieces[0])
    for cut in pieces[1:]:
        loudness = loudness * one(*cut)
    return loudness


def normal_values(own_key, dims, width, reach, pieces=(), kind=jnp.bfloat16):
    factor_of = shard_levels(own_key, dims, pieces, -0.22, 0.18) if pieces else 1.0
    entries = jax.random.normal(own_key, dims, jnp.float32) * width * factor_of
    return jnp.minimum(jnp.maximum(entries, -reach), reach).astype(kind)


def setup_inputs(seed: int = 0) -> dict:
    streams_of = jax.random.split(jax.random.key(seed), 4)
    points = jnp.clip(1.0 * jax.random.uniform(streams_of[0], (NB, 3, M), jnp.float32) ** shard_levels(streams_of[0], (NB, 3, M), ((0, 16),), -0.2, 0.2), 0.0, 1.0).astype(jnp.bfloat16)
    sketch = normal_values(streams_of[1], (NB, M, R), 1.0, 6.0, ((0, 16), (1, 2)))
    near_mask = draw_near_mask(jax.random.fold_in(streams_of[3], 71), 0)
    return dict(points=points, sketch=sketch, near_mask=near_mask)


lift_scale = 0.25

def interaction(row_points, col_points, shift_y, shift_x, first_row, first_col, centre, box_points):
    row_coords = row_points.astype(jnp.float32)
    col_coords = col_points.astype(jnp.float32)
    delta_u = shift_x + col_coords[..., 0, None, :] - row_coords[..., 0, :, None]
    delta_v = shift_y + col_coords[..., 1, None, :] - row_coords[..., 1, :, None]
    delta_w = lift_scale * (col_coords[..., 2, None, :] - row_coords[..., 2, :, None])
    strength = 0.25 / math.sqrt(box_points)
    soften = 0.5 / math.sqrt(box_points)
    values = strength / jnp.sqrt(delta_u * delta_u + delta_v * delta_v + delta_w * delta_w + soften * soften)
    if centre:
        row_ids = first_row + jnp.arange(row_coords.shape[-1], dtype=jnp.int32)
        col_ids = first_col + jnp.arange(col_coords.shape[-1], dtype=jnp.int32)
        values = values + jnp.where(row_ids[:, None] == col_ids[None, :], 1.0, 0.0).astype(jnp.float32)
    return values

def neighbour_table():
    plate_side = TILE * DGRID
    box_ids = jnp.arange(NB, dtype=jnp.int32)
    group_ids = box_ids // (TILE * TILE)
    local_ids = box_ids % (TILE * TILE)
    grid_y = group_ids // DGRID * TILE + local_ids // TILE
    grid_x = group_ids % DGRID * TILE + local_ids % TILE
    columns = []
    for stencil in range(9):
        near_y = jnp.clip(grid_y + (stencil // 3 - 1), 0, plate_side - 1)
        near_x = jnp.clip(grid_x + (stencil % 3 - 1), 0, plate_side - 1)
        near_ids = (near_y // TILE * DGRID + near_x // TILE) * (TILE * TILE) + near_y % TILE * TILE + near_x % TILE
        columns.append(near_ids.astype(jnp.int32))
    return jnp.stack(columns, axis=1)

def orthonormal(sketch_t):
    gram_sum = jnp.einsum('brm,bsm->brs', sketch_t, sketch_t, precision=lax.Precision.HIGHEST) / sketch_t.shape[2]
    lower_factor = jnp.linalg.cholesky(gram_sum)
    identity = jnp.broadcast_to(jnp.eye(gram_sum.shape[1], dtype=gram_sum.dtype), gram_sum.shape)
    inverse_lower = lax.linalg.triangular_solve(lower_factor, identity, left_side=True, lower=True)
    return jnp.einsum('brs,bsm->brm', inverse_lower, sketch_t, precision=lax.Precision.HIGHEST)

def reference(points, sketch, near_mask):
    table_ids = neighbour_table()
    weights = near_mask.astype(jnp.float32)

    def sketch_box(box_index):
        own_coords = points[box_index]
        running = jnp.zeros((M, R), jnp.float32)
        for stencil in range(9):
            near_box = table_ids[box_index, stencil]
            block_vals = interaction(own_coords, points[near_box], stencil // 3 - 1, stencil % 3 - 1, 0, 0, stencil == 4, M).astype(jnp.bfloat16)
            running = running + jnp.dot(block_vals.astype(jnp.float32), sketch[near_box].astype(jnp.float32), preferred_element_type=jnp.float32) * weights[box_index, stencil]
        return running
    sketched = lax.map(sketch_box, jnp.arange(NB, dtype=jnp.int32))
    sketch_t = orthonormal(orthonormal(jnp.transpose(sketched, (0, 2, 1))))
    basis_t = sketch_t.astype(jnp.bfloat16)

    def couple_box(box_index):
        own_coords = points[box_index]
        collected = []
        for stencil in range(9):
            near_box = table_ids[box_index, stencil]
            block_vals = interaction(own_coords, points[near_box], stencil // 3 - 1, stencil % 3 - 1, 0, 0, stencil == 4, M).astype(jnp.bfloat16)
            projected = jnp.dot(basis_t[box_index].astype(jnp.float32), block_vals.astype(jnp.float32), preferred_element_type=jnp.float32).astype(jnp.bfloat16)
            coupling_term = jnp.dot(projected.astype(jnp.float32), jnp.transpose(basis_t[near_box]).astype(jnp.float32), preferred_element_type=jnp.float32) * (1.0 / M) * weights[box_index, stencil]
            collected.append(coupling_term)
        return jnp.stack(collected, axis=0)
    coupling = lax.map(couple_box, jnp.arange(NB, dtype=jnp.int32))
    return (jnp.transpose(basis_t, (0, 2, 1)), coupling)
```

```python
import math

import jax
import jax.numpy as jnp
from jax import lax
from jax.experimental import pallas as pl
from jax.experimental.pallas import tpu as pltpu
from jax.sharding import PartitionSpec as P

lift_scale = 0.25


def shortened(array):

    def short(part):
        return part.astype(jnp.bfloat16) if part.dtype == jnp.float32 else part

    return jax.tree.map(short, array)


def from_behind(value, axis, steps):
    count = lax.axis_size(axis)
    initial, last = (max(0, -steps), min(count, count - steps))
    return lax.ppermute(value, axis, [(source, source + steps) for source in range(initial, last)])


def interaction(row_points, col_points, shift_y, shift_x, centre, box_points):
    row_coords = row_points.astype(jnp.float32)
    col_coords = col_points.astype(jnp.float32)
    delta_u = shift_x + col_coords[..., 0, None, :] - row_coords[..., 0, :, None]
    delta_v = shift_y + col_coords[..., 1, None, :] - row_coords[..., 1, :, None]
    delta_w = lift_scale * (col_coords[..., 2, None, :] - row_coords[..., 2, :, None])
    strength = 0.25 / math.sqrt(box_points)
    soften = 0.5 / math.sqrt(box_points)
    values = strength / jnp.sqrt(
        delta_u * delta_u + delta_v * delta_v + delta_w * delta_w + soften * soften
    )
    if centre:
        row_ids = jnp.arange(row_coords.shape[-1], dtype=jnp.int32)
        col_ids = jnp.arange(col_coords.shape[-1], dtype=jnp.int32)
        values = values + jnp.where(row_ids[:, None] == col_ids[None, :], 1.0, 0.0).astype(
            jnp.float32
        )
    return values


def facing(offset, tile_side):
    if offset == -1:
        return slice(tile_side - 1, tile_side)
    if offset == 1:
        return slice(0, 1)
    return slice(0, tile_side)


def landing(offset, tile_side):
    if offset == -1:
        return slice(0, 1)
    if offset == 1:
        return slice(tile_side + 1, tile_side + 2)
    return slice(1, tile_side + 1)


def neighbours(arrays, tile_side, grid_side):
    extended = [
        jnp.zeros((tile_side + 2, tile_side + 2) + member.shape[2:], member.dtype)
        .at[1 : tile_side + 1, 1 : tile_side + 1]
        .set(member)
        for member in arrays
    ]
    for offset_y in (-1, 0, 1):
        for offset_x in (-1, 0, 1):
            if offset_y == 0 and offset_x == 0:
                continue
            pieces = tuple(
                (
                    member[facing(offset_y, tile_side), facing(offset_x, tile_side)]
                    for member in arrays
                )
            )
            received = jax.tree.map(
                lambda part, own: part.astype(own.dtype),
                from_behind(shortened(pieces), "box", -(offset_y * grid_side + offset_x)),
                pieces,
            )
            extended = [
                holder.at[landing(offset_y, tile_side), landing(offset_x, tile_side)].set(arrived)
                for holder, arrived in zip(extended, received)
            ]
    return extended


def slot_view(extended, row_index, offset_y, offset_x, tile_side):
    row_block = lax.dynamic_index_in_dim(extended, row_index + 1 + offset_y, 0, keepdims=False)
    return row_block[1 + offset_x : 1 + offset_x + tile_side]


PANEL = 8
BLOCK = 32

def lane_copy(value, lane):
    return jnp.broadcast_to(value[:, lane:lane+1], value.shape)

def three_parts(value):
    first = value.astype(jnp.bfloat16)
    rest = value - first.astype(jnp.float32)
    second = rest.astype(jnp.bfloat16)
    third = (rest - second.astype(jnp.float32)).astype(jnp.bfloat16)
    return first, second, third

def factor_panel(rows, base):
    schur = [[lane_copy(rows[base + i], base + j) for j in range(i + 1)] for i in range(PANEL)]
    inverse_pivots, multipliers = [], [[None] * PANEL for _ in range(PANEL)]
    for k in range(PANEL):
        inverse_pivots.append(1.0 / schur[k][k])
        for i in range(k + 1, PANEL):
            multipliers[i][k] = schur[i][k] * inverse_pivots[k]
        for i in range(k + 1, PANEL):
            for j in range(k + 1, i + 1):
                schur[i][j] = schur[i][j] - multipliers[i][k] * schur[j][k]
    unit = [[None] * PANEL for _ in range(PANEL)]
    for i in range(PANEL):
        for j in range(i):
            total = multipliers[i][j]
            for t in range(j + 1, i):
                total = total + multipliers[i][t] * unit[t][j]
            unit[i][j] = -total
    return inverse_pivots, unit

def invert_factors(work, pivots, weights):
    rank, batch, _ = work.shape
    lanes = lax.broadcasted_iota(jnp.int32, (batch, rank), 1)
    square_rows = lax.broadcasted_iota(jnp.int32, (rank, rank), 0)
    square_lanes = lax.broadcasted_iota(jnp.int32, (rank, rank), 1)

    def block_step(block, carry):
        first = block * BLOCK
        back = lax.rem(rank - first, rank)
        rows = [pltpu.roll(work[first + r], back, 1) for r in range(BLOCK)]
        for base in range(0, BLOCK, PANEL):
            inverse_pivots, unit = factor_panel(rows, base)
            inside = (lanes >= base) & (lanes < base + PANEL)
            held_rows, scaled_rows = [], []
            for k in range(PANEL):
                full = rows[base + k]
                for j in range(k):
                    full = full + unit[k][j] * rows[base + j]
                scaled = full * inverse_pivots[k]
                held = jnp.where(inside, 0.0, full)
                for j in range(k):
                    held = jnp.where(lanes == base + j, unit[k][j], held)
                held = jnp.where(lanes == base + k, 1.0, held)
                held_rows.append(held)
                scaled_rows.append(scaled)
            for t in range(base + PANEL, BLOCK):
                row = jnp.where(inside, 0.0, rows[t])
                for k in range(PANEL):
                    row = row - lane_copy(scaled_rows[k], t) * held_rows[k]
                rows[t] = row
            for k in range(PANEL):
                at = base + k
                kept = jnp.where((lanes > at) & (lanes < BLOCK), 0.0, held_rows[k])
                turned = pltpu.roll(kept, first, 1)
                pivots[at] = turned
                weights[at] = pltpu.roll(scaled_rows[k], first, 1)
                work[first + at] = jnp.where(lanes <= first + at, turned, 0.0) * lax.sqrt(inverse_pivots[k])

        @pl.when(first + BLOCK < rank)
        def _():
            below = square_rows >= first + BLOCK
            inside = (square_lanes >= first) & (square_lanes < first + BLOCK)
            for b in range(batch):
                a1, a2, a3 = three_parts(weights[:, b, :])
                b1, b2, b3 = three_parts(pivots[:, b, :])
                left = jnp.concatenate([a1, a1, a2, a2, a1, a3], axis=0)
                right = jnp.concatenate([b1, b2, b1, b2, b3, b1], axis=0)
                change = lax.dot_general(left, right, (((0,), (0,)), ((), ())), preferred_element_type=jnp.float32)
                now = work[:, b, :]
                work[:, b, :] = jnp.where(below, jnp.where(inside, 0.0, now) - change, now)

        return carry

    lax.fori_loop(0, rank // BLOCK, block_step, 0)

def ortho_kernel(y_ref, out_ref, work, held, pivots, weights):
    batch, points, rank = y_ref.shape
    for turn, source in enumerate((y_ref, held)):
        for b in range(batch):
            data = source[b]
            work[:, b, :] = lax.dot_general(data, data, (((0,), (0,)), ((), ())), precision=lax.Precision.HIGHEST, preferred_element_type=jnp.float32) * (1.0 / points)
        invert_factors(work, pivots, weights)
        for b in range(batch):
            data = lax.dot_general(source[b], work[:, b, :], (((1,), (1,)), ((), ())), precision=lax.Precision.HIGHEST, preferred_element_type=jnp.float32)
            if turn == 0:
                held[b] = data
            else:
                out_ref[b] = data.astype(jnp.bfloat16)

def orthonormal(y):
    batch, points, rank = y.shape
    return pl.pallas_call(
        ortho_kernel,
        out_shape=jax.ShapeDtypeStruct(y.shape, jnp.bfloat16),
        in_specs=[pl.BlockSpec(memory_space=pltpu.VMEM)],
        out_specs=pl.BlockSpec(memory_space=pltpu.VMEM),
        scratch_shapes=[pltpu.VMEM((rank, batch, rank), jnp.float32), pltpu.VMEM(y.shape, jnp.float32),
            pltpu.VMEM((BLOCK, batch, rank), jnp.float32), pltpu.VMEM((BLOCK, batch, rank), jnp.float32)],
        compiler_params=pltpu.CompilerParams(vmem_limit_bytes=48 << 20),
        name="orthonormal",
    )(y)


def body(points, sketch, near_mask):
    box_count = points.shape[0]
    tile_side = math.isqrt(box_count)
    grid_side = math.isqrt(lax.axis_size("box"))
    box_points = points.shape[2]
    half_points = sketch.shape[1]
    skel_rank = sketch.shape[2]
    col_index = lax.axis_index("col")
    rows_half = tile_side // lax.axis_size("col")
    own_rows = col_index * rows_half + jnp.arange(rows_half, dtype=jnp.int32)
    weights = near_mask.astype(jnp.float32).reshape(tile_side, tile_side, 9)
    coord_grid = points.reshape(tile_side, tile_side, 3, box_points)
    omega_grid = sketch.reshape(tile_side, tile_side, half_points, skel_rank)
    ext_coords, ext_omega = neighbours((coord_grid, omega_grid), tile_side, grid_side)
    omega_full = lax.all_gather(ext_omega, "col", axis=2, tiled=True)

    def sketch_full(row_index):
        row_coords = lax.dynamic_index_in_dim(coord_grid, row_index, 0, keepdims=False)
        row_weights = lax.dynamic_index_in_dim(weights, row_index, 0, keepdims=False)
        running = jnp.zeros((box_points, tile_side, skel_rank), jnp.float32)
        for stencil in range(9):
            offset_y = stencil // 3 - 1
            offset_x = stencil % 3 - 1
            near_coords = slot_view(ext_coords, row_index, offset_y, offset_x, tile_side)
            near_omega = slot_view(omega_full, row_index, offset_y, offset_x, tile_side)
            block_vals = interaction(
                row_coords, near_coords, offset_y, offset_x, stencil == 4, box_points
            ).astype(jnp.bfloat16)
            running = (
                running
                + jnp.einsum(
                    "bij,bjr->ibr", block_vals, near_omega, preferred_element_type=jnp.float32
                )
                * row_weights[None, :, stencil, None]
            )
        return running

    blocks = lax.map(sketch_full, own_rows)
    sketched = jnp.transpose(blocks, (0, 2, 1, 3)).reshape(
        rows_half * tile_side, box_points, skel_rank
    )
    own_basis = orthonormal(sketched)
    basis_out = lax.all_to_all(own_basis, "col", split_axis=1, concat_axis=0, tiled=True)
    ext_basis = neighbours(
        (basis_out.reshape(tile_side, tile_side, half_points, skel_rank),), tile_side, grid_side
    )[0]
    basis_full = lax.all_gather(ext_basis, "col", axis=2, tiled=True)

    def couple_full(row_index):
        row_coords = lax.dynamic_index_in_dim(coord_grid, row_index, 0, keepdims=False)
        row_weights = lax.dynamic_index_in_dim(weights, row_index, 0, keepdims=False)
        own_basis = slot_view(basis_full, row_index, 0, 0, tile_side)
        collected = []
        for stencil in range(9):
            offset_y = stencil // 3 - 1
            offset_x = stencil % 3 - 1
            near_coords = slot_view(ext_coords, row_index, offset_y, offset_x, tile_side)
            near_basis = slot_view(basis_full, row_index, offset_y, offset_x, tile_side)
            block_vals = interaction(
                row_coords, near_coords, offset_y, offset_x, stencil == 4, box_points
            ).astype(jnp.bfloat16)
            projected = jnp.einsum(
                "bir,bij->brj", own_basis, block_vals, preferred_element_type=jnp.float32
            ).astype(jnp.bfloat16)
            coupling_term = (
                jnp.einsum(
                    "brj,bjs->brs", projected, near_basis, preferred_element_type=jnp.float32
                )
                * (1.0 / box_points)
                * row_weights[:, stencil, None, None]
            )
            collected.append(coupling_term)
        return jnp.stack(collected, axis=1)

    owned = lax.map(couple_full, own_rows).reshape(rows_half * tile_side, 9, skel_rank, skel_rank)
    coupling = lax.all_to_all(owned, "col", split_axis=2, concat_axis=0, tiled=True)
    return (basis_out, coupling)


def solution(mesh):
    return jax.shard_map(
        body,
        mesh=mesh,
        in_specs=(P("box", None, None), P("box", "col", None), P("box", None)),
        out_specs=(P("box", "col", None), P("box", None, "col", None)),
        check_vma=False,
    )
```

```python
import functools
import math

import jax
import jax.numpy as jnp
import numpy as np
from jax import lax
from jax.experimental import pallas as pl
from jax.experimental.pallas import tpu as pltpu
from jax.sharding import PartitionSpec as P

lift_scale = 0.25
LANES = 128
PANEL = 8
BLOCK = 32
VMEM_BYTES = 50 << 20


def lane_copy(value, lane):
    return jnp.broadcast_to(value[:, lane:lane+1], value.shape)

def three_parts(value):
    first = value.astype(jnp.bfloat16)
    rest = value - first.astype(jnp.float32)
    second = rest.astype(jnp.bfloat16)
    third = (rest - second.astype(jnp.float32)).astype(jnp.bfloat16)
    return first, second, third

def factor_panel(rows, base):
    schur = [[lane_copy(rows[base + i], base + j) for j in range(i + 1)] for i in range(PANEL)]
    inverse_pivots, multipliers = [], [[None] * PANEL for _ in range(PANEL)]
    for k in range(PANEL):
        inverse_pivots.append(1.0 / schur[k][k])
        for i in range(k + 1, PANEL):
            multipliers[i][k] = schur[i][k] * inverse_pivots[k]
        for i in range(k + 1, PANEL):
            for j in range(k + 1, i + 1):
                schur[i][j] = schur[i][j] - multipliers[i][k] * schur[j][k]
    unit = [[None] * PANEL for _ in range(PANEL)]
    for i in range(PANEL):
        for j in range(i):
            total = multipliers[i][j]
            for t in range(j + 1, i):
                total = total + multipliers[i][t] * unit[t][j]
            unit[i][j] = -total
    return inverse_pivots, unit

def invert_factors(work, pivots, weights):
    rank, batch, _ = work.shape
    lanes = lax.broadcasted_iota(jnp.int32, (batch, rank), 1)
    square_rows = lax.broadcasted_iota(jnp.int32, (rank, rank), 0)
    square_lanes = lax.broadcasted_iota(jnp.int32, (rank, rank), 1)

    def block_step(block, carry):
        first = block * BLOCK
        back = lax.rem(rank - first, rank)
        rows = [pltpu.roll(work[first + r], back, 1) for r in range(BLOCK)]
        for base in range(0, BLOCK, PANEL):
            inverse_pivots, unit = factor_panel(rows, base)
            inside = (lanes >= base) & (lanes < base + PANEL)
            held_rows, scaled_rows = [], []
            for k in range(PANEL):
                full = rows[base + k]
                for j in range(k):
                    full = full + unit[k][j] * rows[base + j]
                scaled = full * inverse_pivots[k]
                held = jnp.where(inside, 0.0, full)
                for j in range(k):
                    held = jnp.where(lanes == base + j, unit[k][j], held)
                held = jnp.where(lanes == base + k, 1.0, held)
                held_rows.append(held)
                scaled_rows.append(scaled)
            for t in range(base + PANEL, BLOCK):
                row = jnp.where(inside, 0.0, rows[t])
                for k in range(PANEL):
                    row = row - lane_copy(scaled_rows[k], t) * held_rows[k]
                rows[t] = row
            for k in range(PANEL):
                at = base + k
                kept = jnp.where((lanes > at) & (lanes < BLOCK), 0.0, held_rows[k])
                turned = pltpu.roll(kept, first, 1)
                pivots[at] = turned
                weights[at] = pltpu.roll(scaled_rows[k], first, 1)
                work[first + at] = jnp.where(lanes <= first + at, turned, 0.0) * lax.sqrt(inverse_pivots[k])

        @pl.when(first + BLOCK < rank)
        def _():
            below = square_rows >= first + BLOCK
            inside = (square_lanes >= first) & (square_lanes < first + BLOCK)
            for b in range(batch):
                a1, a2, a3 = three_parts(weights[:, b, :])
                b1, b2, b3 = three_parts(pivots[:, b, :])
                left = jnp.concatenate([a1, a1, a2, a2, a1, a3], axis=0)
                right = jnp.concatenate([b1, b2, b1, b2, b3, b1], axis=0)
                change = lax.dot_general(left, right, (((0,), (0,)), ((), ())), preferred_element_type=jnp.float32)
                now = work[:, b, :]
                work[:, b, :] = jnp.where(below, jnp.where(inside, 0.0, now) - change, now)

        return carry

    lax.fori_loop(0, rank // BLOCK, block_step, 0)

def orthonormalize(y_ref, out_ref, work, pivots, weights):
    batch, points, rank = y_ref.shape
    for turn in range(2):
        for b in range(batch):
            data = y_ref[b]
            work[:, b, :] = lax.dot_general(data, data, (((0,), (0,)), ((), ())), precision=lax.Precision.HIGHEST, preferred_element_type=jnp.float32) * (1.0 / points)
        invert_factors(work, pivots, weights)
        for b in range(batch):
            data = lax.dot_general(y_ref[b], work[:, b, :], (((1,), (1,)), ((), ())), precision=lax.Precision.HIGHEST, preferred_element_type=jnp.float32)
            if turn == 0:
                y_ref[b] = data
            else:
                out_ref[b] = data.astype(jnp.bfloat16)


def chip_entries(tile_side, rows_half, core):
    top = core * rows_half
    centres, pairs, singles = [], [], []
    for row in range(rows_half):
        for col in range(tile_side):
            own = row * tile_side + col
            for slot in range(9):
                offset_y, offset_x = slot // 3 - 1, slot % 3 - 1
                other_y, other_x = top + row + offset_y, col + offset_x
                if not (0 <= other_y < tile_side and 0 <= other_x < tile_side):
                    continue
                other = other_y * tile_side + other_x
                mate = other - top * tile_side
                entry = (own, other, offset_y, offset_x, slot, mate)
                if slot == 4:
                    centres.append(entry)
                elif top <= other_y < top + rows_half:
                    if slot > 4:
                        pairs.append(entry)
                else:
                    singles.append(entry[:5] + (-1,))
    return centres, pairs, singles


def edge_entries(tile_side, rows_half, core):
    top = core * rows_half
    corners = 3 * tile_side
    entries = []
    for row in range(rows_half):
        for col in range(tile_side):
            own = row * tile_side + col
            for slot in range(9):
                offset_y, offset_x = slot // 3 - 1, slot % 3 - 1
                other_y, other_x = top + row + offset_y, col + offset_x
                inside_y, inside_x = 0 <= other_y < tile_side, 0 <= other_x < tile_side
                if inside_y and inside_x:
                    continue
                if inside_x:
                    other = 2 * tile_side + other_x
                elif inside_y:
                    other = other_y + (tile_side if other_x > 0 else 0)
                else:
                    other = corners + (0 if (other_y > 0) == (other_x > 0) else 1)
                entries.append((own, other, offset_y, offset_x, slot, -1))
    return entries


def work_lists(tile_side, rows_half, cores):
    chip = [chip_entries(tile_side, rows_half, core) for core in range(cores)]
    edge = [edge_entries(tile_side, rows_half, core) for core in range(cores)]
    counts = tuple(len(part) for part in chip[0])
    flat = [sum(parts, []) for parts in chip]
    return np.array(flat, np.int32), counts, np.array(edge, np.int32)


def spread_points(coords, box_points):
    stretch = math.sqrt(box_points) * 4.0
    return coords.astype(jnp.float32) * stretch


def fill_rows(rows, box_coords, own):
    box_points = box_coords.shape[1]
    turned = jnp.transpose(box_coords)
    for axis in range(3):
        rows[own, axis] = jnp.broadcast_to(turned[:, axis : axis + 1], (box_points, LANES))


def make_entries(target, slot, rows, own, coords, other, offset_y, offset_x, centre, start, stop):
    box_points = coords.shape[2]
    stretch = math.sqrt(box_points) * 4.0
    soften = (0.25 / box_points) * stretch * stretch
    step = 64
    for first in range(start, stop, step):
        for lane in range(0, box_points, LANES):
            here = pl.ds(lane, LANES)
            delta_u = (coords[other, 0:1, here] + offset_x) - rows[own, 0, first : first + step, :]
            delta_v = (coords[other, 1:2, here] + offset_y) - rows[own, 1, first : first + step, :]
            delta_w = coords[other, 2:3, here] - rows[own, 2, first : first + step, :]
            values = lax.rsqrt(delta_u * delta_u + delta_v * delta_v + delta_w * delta_w + soften)
            if centre and lane <= first < lane + LANES:
                row_ids = lax.broadcasted_iota(jnp.int32, values.shape, 0) + (first - lane)
                col_ids = lax.broadcasted_iota(jnp.int32, values.shape, 1)
                values = values + jnp.where(row_ids == col_ids, 1.0, 0.0)
            target[slot, first : first + step, here] = values.astype(jnp.bfloat16)


def list_active(table, core, first, count, mask, active, base):
    def check(index, total):
        on = mask[table[core, first + index, 0], table[core, first + index, 4]] != 0

        @pl.when(on)
        def _():
            active[base + total] = first + index

        return total + jnp.where(on, 1, 0)

    return lax.fori_loop(0, count, check, 0)


def run_blocks(active, base, total, begun, body, buffers, store, sems):
    def step(turn, carry):
        count = begun + turn
        slot = lax.rem(count, 2)

        @pl.when(count >= 2)
        def _():
            pltpu.make_async_copy(buffers.at[slot], store.at[0], sems.at[slot]).wait()

        index = active[base + turn]
        body(index, slot)
        pltpu.make_async_copy(buffers.at[slot], store.at[index], sems.at[slot]).start()
        return carry

    lax.fori_loop(0, total, step, 0)
    return begun + total


def drain(begun, buffers, store, sems):
    for back in (1, 2):

        @pl.when(begun >= back)
        def _():
            slot = lax.rem(begun - back, 2)
            pltpu.make_async_copy(buffers.at[slot], store.at[0], sems.at[slot]).wait()


def place(table, core, index):
    return [table[core, index, field] for field in range(6)]


def chip_sketch_kernel(counts, core_ref, mask, table, points, mine, theirs, y_ref, store,
                       omega, omega_t, coords, rows, turned_y, buffers, active, sems, load_sems):
    core = core_ref[0]
    chip_boxes, _, box_points = points.shape
    own_boxes, _, skel_rank = y_ref.shape
    half = mine.shape[1]
    loads = [
        pltpu.make_async_copy(mine, omega.at[:, pl.ds(pl.multiple_of(core * half, half), half), :], load_sems.at[0]),
        pltpu.make_async_copy(theirs, omega.at[:, pl.ds(pl.multiple_of((1 - core) * half, half), half), :], load_sems.at[1]),
    ]
    for load in loads:
        load.start()
    stretch = math.sqrt(box_points) * 4.0
    for box in range(chip_boxes):
        spread = points[box].astype(jnp.float32) * stretch
        coords[box, 0:2] = spread[0:2]
        coords[box, 2:3] = spread[2:3] * lift_scale
    for own in range(own_boxes):
        fill_rows(rows, coords[core * own_boxes + own], own)
    for load in loads:
        load.wait()
    for own in range(own_boxes):
        omega_t[own] = jnp.transpose(omega[core * own_boxes + own])
        turned_y[own] = jnp.zeros((skel_rank, box_points), jnp.float32)

    part = box_points // 2

    def block(kind, index, slot):
        own, other, offset_y, offset_x, _, mate = place(table, core, index)
        shift_y, shift_x = offset_y.astype(jnp.float32) * stretch, offset_x.astype(jnp.float32) * stretch
        for first in range(0, box_points, part):
            make_entries(buffers, slot, rows, own, coords, other, shift_y, shift_x, kind == 0, first, first + part)
            values = buffers[slot, first : first + part, :]
            found = jnp.dot(values, omega[other], preferred_element_type=jnp.float32)
            if kind == 0:
                y_ref[own, first : first + part, :] = found
            else:
                y_ref[own, first : first + part, :] += found
            if kind == 1:
                turned_y[mate] += jnp.dot(
                    omega_t[own, :, first : first + part], values, preferred_element_type=jnp.float32
                )

    begun, first = 0, 0
    for kind, count in enumerate(counts):
        total = list_active(table, core, first, count, mask, active, first)
        begun = run_blocks(active, first, total, begun, functools.partial(block, kind), buffers, store, sems)
        first += count
    for own in range(own_boxes):
        y_ref[own] += jnp.transpose(turned_y[own])
    drain(begun, buffers, store, sems)


def edge_coords(coords, extended, box, box_points, stretch):
    packed = extended[box, box_points : box_points + 16, :].astype(jnp.float32) * stretch
    strips = box_points // LANES
    for axis in range(3):
        for strip in range(strips):
            row = packed[axis * strips + strip : axis * strips + strip + 1, :]
            coords[box, axis : axis + 1, strip * LANES : (strip + 1) * LANES] = row * lift_scale if axis == 2 else row


def load_edges(core, pieces, extended, sems):
    first_col, second_col, row, corner_a, corner_b = pieces
    side = row.shape[0]
    return [
        pltpu.make_async_copy(first_col, extended.at[pl.ds(core * side, side)], sems.at[0]),
        pltpu.make_async_copy(second_col, extended.at[pl.ds((1 - core) * side, side)], sems.at[1]),
        pltpu.make_async_copy(row, extended.at[pl.ds(2 * side, side)], sems.at[2]),
        pltpu.make_async_copy(corner_a, extended.at[pl.ds(3 * side, 1)], sems.at[3]),
        pltpu.make_async_copy(corner_b, extended.at[pl.ds(3 * side + 1, 1)], sems.at[4]),
    ]


def edge_sketch_kernel(core_ref, mask, table, points, sketched, first_col, second_col, row, corner_a, corner_b,
                       basis, store, extended, coords, rows, y_ref, buffers, active, sems, load_sems,
                       work, pivots, weights):
    core = core_ref[0]
    own_boxes, box_points, skel_rank = y_ref.shape
    loads = load_edges(core, (first_col, second_col, row, corner_a, corner_b), extended, load_sems)
    loads.append(pltpu.make_async_copy(sketched, y_ref, load_sems.at[5]))
    for load in loads:
        load.start()
    stretch = math.sqrt(box_points) * 4.0
    for own in range(own_boxes):
        spread = points[core * own_boxes + own].astype(jnp.float32) * stretch
        coords[0, 0:2] = spread[0:2]
        coords[0, 2:3] = spread[2:3] * lift_scale
        fill_rows(rows, coords[0], own)
    for load in loads:
        load.wait()
    for box in range(extended.shape[0]):
        edge_coords(coords, extended, box, box_points, stretch)
    part = box_points // 2

    def block(index, slot):
        own, other, offset_y, offset_x, _, _ = place(table, core, index)
        shift_y, shift_x = offset_y.astype(jnp.float32) * stretch, offset_x.astype(jnp.float32) * stretch
        for first in range(0, box_points, part):
            make_entries(buffers, slot, rows, own, coords, other, shift_y, shift_x, False, first, first + part)
            values = buffers[slot, first : first + part, :]
            y_ref[own, first : first + part, :] += jnp.dot(
                values, extended[other, 0:box_points, :], preferred_element_type=jnp.float32
            )

    total = list_active(table, core, 0, table.shape[1], mask, active, 0)
    begun = run_blocks(active, 0, total, 0, block, buffers, store, sems)
    orthonormalize(y_ref, basis, work, pivots, weights)
    drain(begun, buffers, store, sems)


def run_stored(active, base, total, buffers, store, sems, depth, body):
    def fetch(turn):
        slot = lax.rem(turn, depth)
        return pltpu.make_async_copy(store.at[active[base + turn]], buffers.at[slot], sems.at[slot])

    for turn in range(depth - 1):

        @pl.when(turn < total)
        def _():
            fetch(turn).start()

    def step(turn, carry):
        @pl.when(turn + depth - 1 < total)
        def _():
            fetch(turn + depth - 1).start()

        fetch(turn).wait()
        body(active[base + turn], lax.rem(turn, depth))
        return carry

    lax.fori_loop(0, total, step, 0)


def chip_couple_kernel(counts, depth, core_ref, mask, table, edge_table, mine, theirs, store, edge_store,
                       keep, give, projected, basis, basis_t, buffers, active, result, sems):
    core = core_ref[0]
    own_boxes, box_points, skel_rank = mine.shape
    half = keep.shape[2]
    basis[pl.ds(core * own_boxes, own_boxes)] = mine[...]
    basis[pl.ds((1 - core) * own_boxes, own_boxes)] = theirs[...]
    for own in range(own_boxes):
        basis_t[own] = jnp.transpose(mine[own])
        keep[own] = jnp.zeros(keep.shape[1:], jnp.float32)
        give[own] = jnp.zeros(give.shape[1:], jnp.float32)

    def put(own, slot, values):
        result[...] = values
        keep[own, slot] = result[pl.ds(pl.multiple_of(core * half, half), half), :]
        give[own, slot] = result[pl.ds(pl.multiple_of((1 - core) * half, half), half), :]

    def block(kind, index, slot):
        own, other, _, _, stencil, mate = place(table, core, index)
        rays = jnp.dot(basis_t[own], buffers[slot], preferred_element_type=jnp.float32).astype(jnp.bfloat16)
        values = jnp.dot(rays, basis[other], preferred_element_type=jnp.float32) * (1.0 / box_points)
        put(own, stencil, values)
        if kind == 1:
            put(mate, 8 - stencil, jnp.transpose(values))

    def edge_block(index, slot):
        own = edge_table[core, index, 0]
        projected[index] = jnp.dot(
            basis_t[own], buffers[slot], preferred_element_type=jnp.float32
        ).astype(jnp.bfloat16)

    first = 0
    for kind, count in enumerate(counts):
        total = list_active(table, core, first, count, mask, active, first)
        run_stored(active, first, total, buffers, store, sems, depth, functools.partial(block, kind))
        first += count
    total = list_active(edge_table, core, 0, edge_table.shape[1], mask, active, 0)
    run_stored(active, 0, total, buffers, edge_store, sems, depth, edge_block)


def edge_couple_kernel(core_ref, mask, edge_table, projected, first_col, second_col, row, corner_a, corner_b,
                       keep_in, give_in, keep, give, extended, results, active, load_sems, sems):
    core = core_ref[0]
    box_points = projected.shape[2]
    half = keep.shape[2]
    loads = load_edges(core, (first_col, second_col, row, corner_a, corner_b), extended, load_sems)
    for load in loads:
        load.start()
    total = list_active(edge_table, core, 0, edge_table.shape[1], mask, active, 0)
    for load in loads:
        load.wait()

    def copies(turn):
        index = active[turn]
        own, stencil = edge_table[core, index, 0], edge_table[core, index, 4]
        mine = results.at[turn, pl.ds(pl.multiple_of(core * half, half), half), :]
        theirs = results.at[turn, pl.ds(pl.multiple_of((1 - core) * half, half), half), :]
        return (
            pltpu.make_async_copy(mine, keep.at[own, stencil], sems.at[turn]),
            pltpu.make_async_copy(theirs, give.at[own, stencil], sems.at[results.shape[0] + turn]),
        )

    def step(turn, carry):
        index = active[turn]
        other = edge_table[core, index, 1]
        results[turn] = jnp.dot(
            projected[index], extended[other], preferred_element_type=jnp.float32
        ) * (1.0 / box_points)
        for copy in copies(turn):
            copy.start()
        return carry

    def finish(turn, carry):
        for copy in copies(turn):
            copy.wait()
        return carry

    lax.fori_loop(0, total, step, 0)
    lax.fori_loop(0, total, finish, 0)


SMEM = pl.BlockSpec(memory_space=pltpu.SMEM)
VMEM = pl.BlockSpec(memory_space=pltpu.VMEM)
ANY = pl.BlockSpec(memory_space=pl.ANY)


def params():
    return pltpu.CompilerParams(vmem_limit_bytes=VMEM_BYTES)


def exchange(boxes, core, grid_side):
    side = boxes.shape[0]

    def send(piece, step_y, step_x):
        pairs = []
        for tile in range(grid_side * grid_side):
            for member in range(2):
                sign = 2 * member - 1
                target_y, target_x = tile // grid_side + sign * step_y, tile % grid_side + sign * step_x
                if 0 <= target_y < grid_side and 0 <= target_x < grid_side:
                    target = target_y * grid_side + target_x
                    pairs.append((tile * 2 + member, target * 2 + 1 - member))
        return lax.ppermute(piece, ("box", "col"), pairs)

    last = side - 1
    low = core == 0
    col = send(jnp.where(low, boxes[:, 0], boxes[:, last]), 0, 1)
    row = send(jnp.where(low, boxes[0], boxes[last]), 1, 0)
    corner_a = send(jnp.where(low, boxes[0, 0:1], boxes[last, last:]), 1, 1)
    corner_b = send(jnp.where(low, boxes[0, last:], boxes[last, 0:1]), 1, -1)
    return col, row, corner_a, corner_b


def swap(value):
    return lax.ppermute(value, "col", [(0, 1), (1, 0)])


def body(points, sketch, near_mask):
    chip_boxes, _, box_points = points.shape
    half_points, skel_rank = sketch.shape[1:]
    tile_side = math.isqrt(chip_boxes)
    grid_side = math.isqrt(lax.axis_size("box"))
    cores = lax.axis_size("col")
    rows_half = tile_side // cores
    own_boxes = rows_half * tile_side
    half_rank = skel_rank // cores
    core = lax.axis_index("col")
    core_arg = core.astype(jnp.int32).reshape(1)
    chip_table, counts, edge_table = work_lists(tile_side, rows_half, cores)
    chip_blocks, edge_blocks = chip_table.shape[1], edge_table.shape[1]
    edge_boxes = 3 * tile_side + 2
    chip_table, edge_table = jnp.asarray(chip_table), jnp.asarray(edge_table)
    own_mask = lax.dynamic_slice_in_dim(near_mask, core * own_boxes, own_boxes, 0)
    low = core == 0

    theirs = swap(sketch)
    packed = points.reshape(chip_boxes, 3 * box_points // skel_rank, skel_rank)
    packed = jnp.pad(packed, ((0, 0), (0, 16 - packed.shape[1]), (0, 0)))
    whole = jnp.where(
        low,
        jnp.concatenate([sketch, theirs, packed], axis=1),
        jnp.concatenate([theirs, sketch, packed], axis=1),
    ).reshape(tile_side, tile_side, box_points + 16, skel_rank)
    col, row, corner_a, corner_b = exchange(whole, core, grid_side)

    bf16, f32 = jnp.bfloat16, jnp.float32
    sketched, store = pl.pallas_call(
        functools.partial(chip_sketch_kernel, counts),
        out_shape=(
            jax.ShapeDtypeStruct((own_boxes, box_points, skel_rank), f32),
            jax.ShapeDtypeStruct((chip_blocks, box_points, box_points), bf16),
        ),
        in_specs=[SMEM, SMEM, SMEM, VMEM, ANY, ANY],
        out_specs=(VMEM, ANY),
        scratch_shapes=[
            pltpu.VMEM((chip_boxes, box_points, skel_rank), bf16),
            pltpu.VMEM((own_boxes, skel_rank, box_points), bf16),
            pltpu.VMEM((chip_boxes, 8, box_points), f32),
            pltpu.VMEM((own_boxes, 3, box_points, LANES), f32),
            pltpu.VMEM((own_boxes, skel_rank, box_points), f32),
            pltpu.VMEM((2, box_points, box_points), bf16),
            pltpu.SMEM((chip_blocks,), jnp.int32),
            pltpu.SemaphoreType.DMA((2,)),
            pltpu.SemaphoreType.DMA((2,)),
        ],
        compiler_params=params(),
        cost_estimate=pl.CostEstimate(flops=8 * 10**9, bytes_accessed=24 * 10**6, transcendentals=0),
        name="chip_sketch",
    )(core_arg, own_mask, chip_table, points, sketch, theirs)

    col, row, corner_a, corner_b, sketched = lax.optimization_barrier((col, row, corner_a, corner_b, sketched))
    second_col = swap(col)
    basis, edge_store = pl.pallas_call(
        edge_sketch_kernel,
        out_shape=(
            jax.ShapeDtypeStruct((own_boxes, box_points, skel_rank), bf16),
            jax.ShapeDtypeStruct((edge_blocks, box_points, box_points), bf16),
        ),
        in_specs=[SMEM, SMEM, SMEM, VMEM] + [ANY] * 6,
        out_specs=(VMEM, ANY),
        scratch_shapes=[
            pltpu.VMEM((edge_boxes, box_points + 16, skel_rank), bf16),
            pltpu.VMEM((edge_boxes, 8, box_points), f32),
            pltpu.VMEM((own_boxes, 3, box_points, LANES), f32),
            pltpu.VMEM((own_boxes, box_points, skel_rank), f32),
            pltpu.VMEM((2, box_points, box_points), bf16),
            pltpu.SMEM((edge_blocks,), jnp.int32),
            pltpu.SemaphoreType.DMA((2,)),
            pltpu.SemaphoreType.DMA((6,)),
            pltpu.VMEM((skel_rank, own_boxes, skel_rank), f32),
            pltpu.VMEM((BLOCK, own_boxes, skel_rank), f32),
            pltpu.VMEM((BLOCK, own_boxes, skel_rank), f32),
        ],
        compiler_params=params(),
        name="edge_sketch",
    )(core_arg, own_mask, edge_table, points, sketched, col, second_col, row, corner_a, corner_b)

    other_basis = swap(basis)
    whole = jnp.where(
        low,
        jnp.concatenate([basis, other_basis], axis=0),
        jnp.concatenate([other_basis, basis], axis=0),
    ).reshape(tile_side, tile_side, box_points, skel_rank)
    col, row, corner_a, corner_b = exchange(whole, core, grid_side)
    depth = 4
    coupling_shape = jax.ShapeDtypeStruct((own_boxes, 9, half_rank, skel_rank), f32)
    keep, give, projected = pl.pallas_call(
        functools.partial(chip_couple_kernel, counts, depth),
        out_shape=(
            coupling_shape,
            coupling_shape,
            jax.ShapeDtypeStruct((edge_blocks, skel_rank, box_points), bf16),
        ),
        in_specs=[SMEM] * 4 + [VMEM, VMEM, ANY, ANY],
        out_specs=(VMEM, VMEM, VMEM),
        scratch_shapes=[
            pltpu.VMEM((chip_boxes, box_points, skel_rank), bf16),
            pltpu.VMEM((own_boxes, skel_rank, box_points), bf16),
            pltpu.VMEM((depth, box_points, box_points), bf16),
            pltpu.SMEM((max(chip_blocks, edge_blocks),), jnp.int32),
            pltpu.VMEM((skel_rank, skel_rank), f32),
            pltpu.SemaphoreType.DMA((depth,)),
        ],
        compiler_params=params(),
        cost_estimate=pl.CostEstimate(flops=8 * 10**9, bytes_accessed=32 * 10**6, transcendentals=0),
        name="chip_couple",
    )(core_arg, own_mask, chip_table, edge_table, basis, other_basis, store, edge_store)

    col, row, corner_a, corner_b, projected = lax.optimization_barrier((col, row, corner_a, corner_b, projected))
    second_col = swap(col)
    keep, give = pl.pallas_call(
        edge_couple_kernel,
        out_shape=(coupling_shape, coupling_shape),
        in_specs=[SMEM] * 3 + [VMEM] + [ANY] * 7,
        out_specs=(ANY, ANY),
        scratch_shapes=[
            pltpu.VMEM((edge_boxes, box_points, skel_rank), bf16),
            pltpu.VMEM((edge_blocks, skel_rank, skel_rank), f32),
            pltpu.SMEM((edge_blocks,), jnp.int32),
            pltpu.SemaphoreType.DMA((5,)),
            pltpu.SemaphoreType.DMA((2 * edge_blocks,)),
        ],
        input_output_aliases={9: 0, 10: 1},
        compiler_params=params(),
        name="edge_couple",
    )(core_arg, own_mask, edge_table, projected, col, second_col, row, corner_a, corner_b, keep, give)

    taken = swap(give)
    coupling = jnp.where(low, jnp.concatenate([keep, taken], axis=0), jnp.concatenate([taken, keep], axis=0))
    basis_out = lax.dynamic_slice_in_dim(
        whole.reshape(chip_boxes, box_points, skel_rank), core * half_points, half_points, 1
    )
    return basis_out, coupling


def solution(mesh):
    return jax.shard_map(
        body,
        mesh=mesh,
        in_specs=(P("box", None, None), P("box", "col", None), P("box", None)),
        out_specs=(P("box", "col", None), P("box", None, "col", None)),
        check_vma=False,
    )
```

```python
import functools
import math

import jax
import jax.numpy as jnp
import numpy as np
from jax import lax
from jax.experimental import pallas as pl
from jax.experimental.pallas import tpu as pltpu
from jax.sharding import PartitionSpec as P

lift_scale = 0.25
LANES = 128
PANEL = 8
BLOCK = 32


def lane_copy(value, lane):
    return jnp.broadcast_to(value[:, lane:lane+1], value.shape)

def three_parts(value):
    first = value.astype(jnp.bfloat16)
    rest = value - first.astype(jnp.float32)
    second = rest.astype(jnp.bfloat16)
    third = (rest - second.astype(jnp.float32)).astype(jnp.bfloat16)
    return first, second, third

def factor_panel(rows, base):
    schur = [[lane_copy(rows[base + i], base + j) for j in range(i + 1)] for i in range(PANEL)]
    inverse_pivots, multipliers = [], [[None] * PANEL for _ in range(PANEL)]
    for k in range(PANEL):
        inverse_pivots.append(1.0 / schur[k][k])
        for i in range(k + 1, PANEL):
            multipliers[i][k] = schur[i][k] * inverse_pivots[k]
        for i in range(k + 1, PANEL):
            for j in range(k + 1, i + 1):
                schur[i][j] = schur[i][j] - multipliers[i][k] * schur[j][k]
    unit = [[None] * PANEL for _ in range(PANEL)]
    for i in range(PANEL):
        for j in range(i):
            total = multipliers[i][j]
            for t in range(j + 1, i):
                total = total + multipliers[i][t] * unit[t][j]
            unit[i][j] = -total
    return inverse_pivots, unit

def invert_factors(work, pivots, weights):
    rank, batch, _ = work.shape
    lanes = lax.broadcasted_iota(jnp.int32, (batch, rank), 1)
    square_rows = lax.broadcasted_iota(jnp.int32, (rank, rank), 0)
    square_lanes = lax.broadcasted_iota(jnp.int32, (rank, rank), 1)

    def block_step(block, carry):
        first = block * BLOCK
        back = lax.rem(rank - first, rank)
        rows = [pltpu.roll(work[first + r], back, 1) for r in range(BLOCK)]
        for base in range(0, BLOCK, PANEL):
            inverse_pivots, unit = factor_panel(rows, base)
            inside = (lanes >= base) & (lanes < base + PANEL)
            held_rows, scaled_rows = [], []
            for k in range(PANEL):
                full = rows[base + k]
                for j in range(k):
                    full = full + unit[k][j] * rows[base + j]
                scaled = full * inverse_pivots[k]
                held = jnp.where(inside, 0.0, full)
                for j in range(k):
                    held = jnp.where(lanes == base + j, unit[k][j], held)
                held = jnp.where(lanes == base + k, 1.0, held)
                held_rows.append(held)
                scaled_rows.append(scaled)
            for t in range(base + PANEL, BLOCK):
                row = jnp.where(inside, 0.0, rows[t])
                for k in range(PANEL):
                    row = row - lane_copy(scaled_rows[k], t) * held_rows[k]
                rows[t] = row
            for k in range(PANEL):
                at = base + k
                kept = jnp.where((lanes > at) & (lanes < BLOCK), 0.0, held_rows[k])
                turned = pltpu.roll(kept, first, 1)
                pivots[at] = turned
                weights[at] = pltpu.roll(scaled_rows[k], first, 1)
                work[first + at] = jnp.where(lanes <= first + at, turned, 0.0) * lax.sqrt(inverse_pivots[k])

        @pl.when(first + BLOCK < rank)
        def _():
            below = square_rows >= first + BLOCK
            inside = (square_lanes >= first) & (square_lanes < first + BLOCK)
            changes = []
            for b in range(batch):
                a1, a2, a3 = three_parts(weights[:, b, :])
                b1, b2, b3 = three_parts(pivots[:, b, :])
                left = jnp.concatenate([a1, a1, a2, a2, a1, a3], axis=0)
                right = jnp.concatenate([b1, b2, b1, b2, b3, b1], axis=0)
                changes.append(lax.dot_general(left, right, (((0,), (0,)), ((), ())), preferred_element_type=jnp.float32))
            for b in range(batch):
                now = work[:, b, :]
                work[:, b, :] = jnp.where(below, jnp.where(inside, 0.0, now) - changes[b], now)

        return carry

    lax.fori_loop(0, rank // BLOCK, block_step, 0)

def orthonormalize(y_ref, out_ref, work, pivots, weights):
    batch, points, rank = y_ref.shape
    for turn in range(2):
        grams = []
        for b in range(batch):
            data = y_ref[b]
            grams.append(lax.dot_general(data, data, (((0,), (0,)), ((), ())), precision=lax.Precision.HIGHEST, preferred_element_type=jnp.float32) * (1.0 / points))
        for b in range(batch):
            work[:, b, :] = grams[b]
        invert_factors(work, pivots, weights)
        for b in range(batch):
            data = lax.dot_general(y_ref[b], work[:, b, :], (((1,), (1,)), ((), ())), precision=lax.Precision.HIGHEST, preferred_element_type=jnp.float32)
            if turn == 0:
                y_ref[b] = data
            else:
                out_ref[b] = data.astype(jnp.bfloat16)


def chip_entries(tile_side, rows_half, core):
    top = core * rows_half
    centres, pairs, singles = [], [], []
    for row in range(rows_half):
        for col in range(tile_side):
            own = row * tile_side + col
            for slot in range(9):
                offset_y, offset_x = slot // 3 - 1, slot % 3 - 1
                other_y, other_x = top + row + offset_y, col + offset_x
                if not (0 <= other_y < tile_side and 0 <= other_x < tile_side):
                    continue
                other = other_y * tile_side + other_x
                mate = other - top * tile_side
                entry = (own, other, offset_y, offset_x, slot, mate)
                if slot == 4:
                    centres.append(entry)
                elif top <= other_y < top + rows_half:
                    if slot > 4:
                        pairs.append(entry)
                else:
                    singles.append(entry[:5] + (-1,))
    return centres, pairs, singles


def edge_entries(tile_side, rows_half, core):
    top = core * rows_half
    corners = 3 * tile_side
    entries = []
    for row in range(rows_half):
        for col in range(tile_side):
            own = row * tile_side + col
            for slot in range(9):
                offset_y, offset_x = slot // 3 - 1, slot % 3 - 1
                other_y, other_x = top + row + offset_y, col + offset_x
                inside_y, inside_x = 0 <= other_y < tile_side, 0 <= other_x < tile_side
                if inside_y and inside_x:
                    continue
                if inside_x:
                    other = 2 * tile_side + other_x
                elif inside_y:
                    other = other_y + (tile_side if other_x > 0 else 0)
                else:
                    other = corners + (0 if (other_y > 0) == (other_x > 0) else 1)
                entries.append((own, other, offset_y, offset_x, slot, -1))
    return entries


def work_lists(tile_side, rows_half, cores):
    chip = [chip_entries(tile_side, rows_half, core) for core in range(cores)]
    edge = [edge_entries(tile_side, rows_half, core) for core in range(cores)]
    chip = [(centres + singles, pairs) for centres, pairs, singles in chip]
    counts = tuple(len(part) for part in chip[0])
    flat = [sum(parts, []) for parts in chip]
    return np.array(flat, np.int32), counts, np.array(edge, np.int32)


def fill_coords(coords, place, box_coords, stretch):
    moved = (box_coords - 0.5) * stretch
    coords[place, 0:2] = moved[0:2]
    coords[place, 2:3] = moved[2:3] * lift_scale


def fill_rows(rows, box_coords, own, soften):
    box_points = box_coords.shape[1]
    turned = jnp.transpose(box_coords)
    total = soften
    for axis in range(3):
        column = jnp.broadcast_to(turned[:, axis : axis + 1], (box_points, LANES))
        rows[own, axis] = column + column
        total = total + column * column
    rows[own, 3] = total


def make_entries(target, rows, own, coords, other, shift_y, shift_x):
    box_points = coords.shape[2]
    step = 16
    columns = []
    for lane in range(0, box_points, LANES):
        here = pl.ds(lane, LANES)
        other_u = coords[other, 0:1, here] + shift_x
        other_v = coords[other, 1:2, here] + shift_y
        other_w = coords[other, 2:3, here]
        squares = other_u * other_u + other_v * other_v + other_w * other_w
        columns.append([jnp.broadcast_to(value, (step, LANES)) for value in (other_u, other_v, other_w, squares)])
    for first in range(0, box_points, step):
        part = slice(first, first + step)
        row_u, row_v, row_w, row_squares = (rows[own, axis, part, :] for axis in range(4))
        for strip, (other_u, other_v, other_w, squares) in enumerate(columns):
            apart = (row_squares + squares) - row_u * other_u - row_v * other_v - row_w * other_w
            target[part, strip * LANES : (strip + 1) * LANES] = lax.rsqrt(apart).astype(jnp.bfloat16)


def list_active(table, core, first, count, mask, active, base):
    def check(index, total):
        on = mask[table[core, first + index, 0], table[core, first + index, 4]] != 0

        @pl.when(on)
        def _():
            active[base + total] = first + index

        return total + jnp.where(on, 1, 0)

    return lax.fori_loop(0, count, check, 0)


def run_blocks(active, base, total, make, use, store, pair, sems):
    def entry(turn):
        return active[base + jnp.minimum(turn, total - 1)]

    def send(side, slot, turn):
        return pltpu.make_async_copy(pair[side].at[slot], store.at[entry(turn)], sems.at[side, slot])

    @pl.when(total > 0)
    def _():
        make(entry(0), pair[0].at[0])
        send(0, 0, 0).start()

    def step(half_turn, carry):
        even = 2 * half_turn
        odd, after = even + 1, even + 2
        slot = lax.rem(half_turn, 2)

        @pl.when(half_turn > 1)
        def _():
            send(1, slot, 0).wait()

        make(entry(odd), pair[1].at[slot])
        use(entry(even), pair[0].at[slot], 1.0)

        @pl.when(odd < total)
        def _():
            send(1, slot, odd).start()

        @pl.when(half_turn > 0)
        def _():
            send(0, 1 - slot, 0).wait()

        make(entry(after), pair[0].at[1 - slot])
        use(entry(odd), pair[1].at[slot], jnp.where(odd < total, 1.0, 0.0))

        @pl.when(after < total)
        def _():
            send(0, 1 - slot, after).start()

        return carry

    turns = (total + 1) // 2
    lax.fori_loop(0, turns, step, 0)

    @pl.when(turns > 0)
    def _():
        send(0, lax.rem(turns - 1, 2), 0).wait()

    @pl.when(turns > 1)
    def _():
        send(1, lax.rem(turns, 2), 0).wait()

    @pl.when((turns > 0) & (2 * turns == total))
    def _():
        send(1, lax.rem(turns - 1, 2), 0).wait()


def place(table, core, index):
    return [table[core, index, field] for field in range(6)]


def chip_sketch_kernel(counts, core_ref, mask, table, points, mine, theirs, y_ref, store,
                       omega, omega_t, coords, rows, turned_y, buffer_a, buffer_b, active, sems, load_sems):
    core = core_ref[0]
    chip_boxes, _, box_points = points.shape
    own_boxes, _, skel_rank = y_ref.shape
    half = mine.shape[1]
    loads = [
        pltpu.make_async_copy(mine, omega.at[:, pl.ds(pl.multiple_of(core * half, half), half), :], load_sems.at[0]),
        pltpu.make_async_copy(theirs, omega.at[:, pl.ds(pl.multiple_of((1 - core) * half, half), half), :], load_sems.at[1]),
    ]
    for load in loads:
        load.start()
    stretch = math.sqrt(box_points) * 4.0
    soften = (0.25 / box_points) * stretch * stretch
    for box in range(chip_boxes):
        fill_coords(coords, box, points[box].astype(jnp.float32), stretch)
    for own in range(own_boxes):
        fill_rows(rows, coords[core * own_boxes + own], own, soften)
    for load in loads:
        load.wait()
    for own in range(own_boxes):
        values = omega[core * own_boxes + own]
        omega_t[own] = jnp.transpose(values)
        y_ref[own] = values.astype(jnp.float32)
        turned_y[own] = jnp.zeros((skel_rank, box_points), jnp.float32)

    def make(index, target):
        own, other, offset_y, offset_x, _, _ = place(table, core, index)
        shift_y, shift_x = offset_y.astype(jnp.float32) * stretch, offset_x.astype(jnp.float32) * stretch
        make_entries(target, rows, own, coords, other, shift_y, shift_x)

    def use(both, index, buffer, weight):
        own, other, _, _, _, mate = place(table, core, index)
        values = buffer[...]
        y_ref[own] += jnp.dot(values, omega[other], preferred_element_type=jnp.float32) * weight
        if both:
            turned_y[mate] += jnp.dot(omega_t[own], values, preferred_element_type=jnp.float32) * weight

    first = 0
    for both, count in enumerate(counts):
        total = list_active(table, core, first, count, mask, active, first)
        run_blocks(active, first, total, make, functools.partial(use, both), store, (buffer_a, buffer_b), sems)
        first += count
    for own in range(own_boxes):
        y_ref[own] += jnp.transpose(turned_y[own])


def edge_coords(coords, extended, box, box_points, stretch):
    packed = (extended[box, box_points : box_points + 16, :].astype(jnp.float32) - 0.5) * stretch
    strips = box_points // LANES
    for axis in range(3):
        for strip in range(strips):
            row = packed[axis * strips + strip : axis * strips + strip + 1, :]
            coords[box, axis : axis + 1, strip * LANES : (strip + 1) * LANES] = row * lift_scale if axis == 2 else row


def load_edges(core, pieces, extended, sems):
    first_col, second_col, row, corner_a, corner_b = pieces
    side = row.shape[0]
    return [
        pltpu.make_async_copy(first_col, extended.at[pl.ds(core * side, side)], sems.at[0]),
        pltpu.make_async_copy(second_col, extended.at[pl.ds((1 - core) * side, side)], sems.at[1]),
        pltpu.make_async_copy(row, extended.at[pl.ds(2 * side, side)], sems.at[2]),
        pltpu.make_async_copy(corner_a, extended.at[pl.ds(3 * side, 1)], sems.at[3]),
        pltpu.make_async_copy(corner_b, extended.at[pl.ds(3 * side + 1, 1)], sems.at[4]),
    ]


def edge_sketch_kernel(core_ref, mask, table, points, sketched, first_col, second_col, row, corner_a, corner_b,
                       basis, store, extended, coords, rows, y_ref, buffer_a, buffer_b, active, sems, load_sems,
                       work, pivots, weights):
    core = core_ref[0]
    own_boxes, box_points, skel_rank = y_ref.shape
    loads = load_edges(core, (first_col, second_col, row, corner_a, corner_b), extended, load_sems)
    loads.append(pltpu.make_async_copy(sketched, y_ref, load_sems.at[5]))
    for load in loads:
        load.start()
    stretch = math.sqrt(box_points) * 4.0
    soften = (0.25 / box_points) * stretch * stretch
    for own in range(own_boxes):
        fill_coords(coords, own, points[core * own_boxes + own].astype(jnp.float32), stretch)
        fill_rows(rows, coords[own], own, soften)
    for load in loads:
        load.wait()
    for box in range(extended.shape[0]):
        edge_coords(coords, extended, box, box_points, stretch)

    def make(index, target):
        own, other, offset_y, offset_x, _, _ = place(table, core, index)
        shift_y, shift_x = offset_y.astype(jnp.float32) * stretch, offset_x.astype(jnp.float32) * stretch
        make_entries(target, rows, own, coords, other, shift_y, shift_x)

    def use(index, buffer, weight):
        own, other, _, _, _, _ = place(table, core, index)
        y_ref[own] += jnp.dot(
            buffer[...], extended[other, 0:box_points, :], preferred_element_type=jnp.float32
        ) * weight

    total = list_active(table, core, 0, table.shape[1], mask, active, 0)
    run_blocks(active, 0, total, make, use, store, (buffer_a, buffer_b), sems)
    orthonormalize(y_ref, basis, work, pivots, weights)


def run_stored(active, base, total, buffers, store, sems, depth, project, use, pair):
    def entry(turn):
        return active[base + jnp.minimum(turn, total - 1)]

    def fetch(turn):
        slot = lax.rem(turn, depth)
        return pltpu.make_async_copy(store.at[active[base + turn]], buffers.at[slot], sems.at[slot])

    def arrive(turn, side):
        @pl.when(turn < total)
        def _():
            fetch(turn).wait()

        project(entry(turn), lax.rem(jnp.minimum(turn, total - 1), depth), pair[side])

    for turn in range(depth - 1):

        @pl.when(turn < total)
        def _():
            fetch(turn).start()

    @pl.when(total > 0)
    def _():
        arrive(0, 0)

    def step(half_turn, carry):
        even = 2 * half_turn
        for ahead in (0, 1):

            @pl.when(even + ahead + depth - 1 < total)
            def _():
                fetch(even + ahead + depth - 1).start()

            arrive(even + ahead + 1, 1 - ahead)
            use(entry(even + ahead), pair[ahead])
        return carry

    lax.fori_loop(0, (total + 1) // 2, step, 0)


def chip_couple_kernel(counts, depth, core_ref, mask, table, edge_table, mine, theirs, store, edge_store,
                       full, give, projected, basis, basis_t, buffers, active, found, ray_a, ray_b, sems, out_sems):
    core = core_ref[0]
    own_boxes, box_points, skel_rank = mine.shape
    half = give.shape[2]
    basis[pl.ds(core * own_boxes, own_boxes)] = mine[...]
    basis[pl.ds((1 - core) * own_boxes, own_boxes)] = theirs[...]
    for own in range(own_boxes):
        basis_t[own] = jnp.transpose(mine[own])

    def clear(index, carry):
        own, stencil = index // 9, lax.rem(index, 9)

        @pl.when(mask[own, stencil] == 0)
        def _():
            found[own, stencil] = jnp.zeros((skel_rank, skel_rank), jnp.float32)

        return carry

    lax.fori_loop(0, own_boxes * 9, clear, 0)

    def project(index, slot, target):
        own, stencil = table[core, index, 0], table[core, index, 4]
        centre = jnp.where(stencil == 4, 1.0, 0.0)
        values = jnp.dot(basis_t[own], buffers[slot], preferred_element_type=jnp.float32)
        target[...] = (values + basis_t[own].astype(jnp.float32) * centre).astype(jnp.bfloat16)

    def use(both, index, rays):
        own, other, _, _, stencil, mate = place(table, core, index)
        values = jnp.dot(rays[...], basis[other], preferred_element_type=jnp.float32) * (1.0 / box_points)
        found[own, stencil] = values
        if both:
            found[mate, 8 - stencil] = jnp.transpose(values)

    first = 0
    for both, count in enumerate(counts):
        total = list_active(table, core, first, count, mask, active, first)
        run_stored(active, first, total, buffers, store, sems, depth, project, functools.partial(use, both), (ray_a, ray_b))
        first += count

    copies = []
    for own in range(own_boxes):
        for side, (target, at) in enumerate(((full, core * own_boxes + own), (give, own))):
            rows_of = core if side == 0 else 1 - core
            copies.append(pltpu.make_async_copy(
                found.at[own, :, pl.ds(pl.multiple_of(rows_of * half, half), half), :],
                target.at[at],
                out_sems.at[2 * own + side],
            ))
    for copy in copies:
        copy.start()

    def edge_project(index, slot, target):
        own = edge_table[core, index, 0]
        projected[index] = jnp.dot(
            basis_t[own], buffers[slot], preferred_element_type=jnp.float32
        ).astype(jnp.bfloat16)

    total = list_active(edge_table, core, 0, edge_table.shape[1], mask, active, 0)
    run_stored(active, 0, total, buffers, edge_store, sems, depth, edge_project, lambda index, rays: None, (ray_a, ray_b))
    for copy in copies:
        copy.wait()


def edge_couple_kernel(core_ref, mask, edge_table, projected, first_col, second_col, row, corner_a, corner_b,
                       taken, full_in, full, give, extended, results, active, load_sems, sems, move_sems):
    core = core_ref[0]
    box_points = projected.shape[2]
    own_boxes, _, half, _ = taken.shape
    loads = load_edges(core, (first_col, second_col, row, corner_a, corner_b), extended, load_sems)
    moves = [
        pltpu.make_async_copy(taken.at[own], full.at[(1 - core) * own_boxes + own], move_sems.at[own])
        for own in range(own_boxes)
    ]
    for copy in loads + moves:
        copy.start()
    total = list_active(edge_table, core, 0, edge_table.shape[1], mask, active, 0)
    for load in loads:
        load.wait()

    def result_copy(turn):
        index = active[turn]
        own, stencil = edge_table[core, index, 0], edge_table[core, index, 4]
        mine = results.at[turn, pl.ds(pl.multiple_of(core * half, half), half), :]
        return pltpu.make_async_copy(mine, full.at[core * own_boxes + own, stencil], sems.at[turn])

    def step(turn, carry):
        index = active[turn]
        results[turn] = jnp.dot(
            projected[index], extended[edge_table[core, index, 1]], preferred_element_type=jnp.float32
        ) * (1.0 / box_points)
        give[index] = results[turn, pl.ds(pl.multiple_of((1 - core) * half, half), half), :]
        result_copy(turn).start()
        return carry

    def finish(turn, carry):
        result_copy(turn).wait()
        return carry

    lax.fori_loop(0, total, step, 0)
    lax.fori_loop(0, total, finish, 0)
    for move in moves:
        move.wait()


def settle_kernel(core_ref, mask, edge_table, taken, full_in, full, sems):
    other = 1 - core_ref[0]
    own_boxes = full.shape[0] // 2

    def each(act):
        def step(index, carry):
            own, stencil = edge_table[other, index, 0], edge_table[other, index, 4]

            @pl.when(mask[other * own_boxes + own, stencil] != 0)
            def _():
                act(pltpu.make_async_copy(
                    taken.at[index], full.at[other * own_boxes + own, stencil], sems.at[index]
                ))

            return carry

        lax.fori_loop(0, edge_table.shape[1], step, 0)

    each(lambda copy: copy.start())
    each(lambda copy: copy.wait())


SMEM = pl.BlockSpec(memory_space=pltpu.SMEM)
VMEM = pl.BlockSpec(memory_space=pltpu.VMEM)
ANY = pl.BlockSpec(memory_space=pl.ANY)
HBM = pl.BlockSpec(memory_space=pltpu.HBM)


def params(mebibytes):
    return pltpu.CompilerParams(vmem_limit_bytes=mebibytes << 20)


def exchange(boxes, core, grid_side):
    side = boxes.shape[0]

    def send(piece, step_y, step_x):
        pairs = []
        for tile in range(grid_side * grid_side):
            for member in range(2):
                sign = 2 * member - 1
                target_y, target_x = tile // grid_side + sign * step_y, tile % grid_side + sign * step_x
                if 0 <= target_y < grid_side and 0 <= target_x < grid_side:
                    target = target_y * grid_side + target_x
                    pairs.append((tile * 2 + member, target * 2 + 1 - member))
        return lax.ppermute(piece, ("box", "col"), pairs)

    last = side - 1
    low = core == 0
    col = send(jnp.where(low, boxes[:, 0], boxes[:, last]), 0, 1)
    row = send(jnp.where(low, boxes[0], boxes[last]), 1, 0)
    corner_a = send(jnp.where(low, boxes[0, 0:1], boxes[last, last:]), 1, 1)
    corner_b = send(jnp.where(low, boxes[0, last:], boxes[last, 0:1]), 1, -1)
    return col, row, corner_a, corner_b


def swap(value):
    return lax.ppermute(value, "col", [(0, 1), (1, 0)])


def body(points, sketch, near_mask):
    chip_boxes, _, box_points = points.shape
    half_points, skel_rank = sketch.shape[1:]
    tile_side = math.isqrt(chip_boxes)
    grid_side = math.isqrt(lax.axis_size("box"))
    cores = lax.axis_size("col")
    rows_half = tile_side // cores
    own_boxes = rows_half * tile_side
    half_rank = skel_rank // cores
    core = lax.axis_index("col")
    core_arg = core.astype(jnp.int32).reshape(1)
    chip_table, counts, edge_table = work_lists(tile_side, rows_half, cores)
    chip_blocks, edge_blocks = chip_table.shape[1], edge_table.shape[1]
    edge_boxes = 3 * tile_side + 2
    chip_table, edge_table = jnp.asarray(chip_table), jnp.asarray(edge_table)
    own_mask = lax.dynamic_slice_in_dim(near_mask, core * own_boxes, own_boxes, 0)
    low = core == 0

    theirs = swap(sketch)
    packed = points.reshape(chip_boxes, 3 * box_points // skel_rank, skel_rank)
    packed = jnp.pad(packed, ((0, 0), (0, 16 - packed.shape[1]), (0, 0)))
    whole = jnp.where(
        low,
        jnp.concatenate([sketch, theirs, packed], axis=1),
        jnp.concatenate([theirs, sketch, packed], axis=1),
    ).reshape(tile_side, tile_side, box_points + 16, skel_rank)
    col, row, corner_a, corner_b = exchange(whole, core, grid_side)

    bf16, f32 = jnp.bfloat16, jnp.float32
    sketched, store = pl.pallas_call(
        functools.partial(chip_sketch_kernel, counts),
        out_shape=(
            jax.ShapeDtypeStruct((own_boxes, box_points, skel_rank), f32),
            jax.ShapeDtypeStruct((chip_blocks, box_points, box_points), bf16),
        ),
        in_specs=[SMEM, SMEM, SMEM, VMEM, ANY, ANY],
        out_specs=(VMEM, HBM),
        scratch_shapes=[
            pltpu.VMEM((chip_boxes, box_points, skel_rank), bf16),
            pltpu.VMEM((own_boxes, skel_rank, box_points), bf16),
            pltpu.VMEM((chip_boxes, 8, box_points), f32),
            pltpu.VMEM((own_boxes, 4, box_points, LANES), f32),
            pltpu.VMEM((own_boxes, skel_rank, box_points), f32),
            pltpu.VMEM((2, box_points, box_points), bf16),
            pltpu.VMEM((2, box_points, box_points), bf16),
            pltpu.SMEM((chip_blocks,), jnp.int32),
            pltpu.SemaphoreType.DMA((2, 2)),
            pltpu.SemaphoreType.DMA((2,)),
        ],
        compiler_params=params(50),
        cost_estimate=pl.CostEstimate(flops=8 * 10**9, bytes_accessed=24 * 10**6, transcendentals=0),
        name="chip_sketch",
    )(core_arg, own_mask, chip_table, points, sketch, theirs)

    col, row, corner_a, corner_b, sketched = lax.optimization_barrier((col, row, corner_a, corner_b, sketched))
    second_col = swap(col)
    basis, edge_store = pl.pallas_call(
        edge_sketch_kernel,
        out_shape=(
            jax.ShapeDtypeStruct((own_boxes, box_points, skel_rank), bf16),
            jax.ShapeDtypeStruct((edge_blocks, box_points, box_points), bf16),
        ),
        in_specs=[SMEM, SMEM, SMEM, VMEM] + [ANY] * 6,
        out_specs=(VMEM, ANY),
        scratch_shapes=[
            pltpu.VMEM((edge_boxes, box_points + 16, skel_rank), bf16),
            pltpu.VMEM((edge_boxes, 8, box_points), f32),
            pltpu.VMEM((own_boxes, 4, box_points, LANES), f32),
            pltpu.VMEM((own_boxes, box_points, skel_rank), f32),
            pltpu.VMEM((2, box_points, box_points), bf16),
            pltpu.VMEM((2, box_points, box_points), bf16),
            pltpu.SMEM((edge_blocks,), jnp.int32),
            pltpu.SemaphoreType.DMA((2, 2)),
            pltpu.SemaphoreType.DMA((6,)),
            pltpu.VMEM((skel_rank, own_boxes, skel_rank), f32),
            pltpu.VMEM((BLOCK, own_boxes, skel_rank), f32),
            pltpu.VMEM((BLOCK, own_boxes, skel_rank), f32),
        ],
        compiler_params=params(24),
        name="edge_sketch",
    )(core_arg, own_mask, edge_table, points, sketched, col, second_col, row, corner_a, corner_b)

    other_basis = swap(basis)
    whole = jnp.where(
        low,
        jnp.concatenate([basis, other_basis], axis=0),
        jnp.concatenate([other_basis, basis], axis=0),
    ).reshape(tile_side, tile_side, box_points, skel_rank)
    col, row, corner_a, corner_b = exchange(whole, core, grid_side)
    depth = 8
    coupling_shape = jax.ShapeDtypeStruct((chip_boxes, 9, half_rank, skel_rank), f32)
    coupling, give, projected = pl.pallas_call(
        functools.partial(chip_couple_kernel, counts, depth),
        out_shape=(
            coupling_shape,
            jax.ShapeDtypeStruct((own_boxes, 9, half_rank, skel_rank), f32),
            jax.ShapeDtypeStruct((edge_blocks, skel_rank, box_points), bf16),
        ),
        in_specs=[SMEM] * 4 + [VMEM, VMEM, HBM, ANY],
        out_specs=(ANY, ANY, VMEM),
        scratch_shapes=[
            pltpu.VMEM((chip_boxes, box_points, skel_rank), bf16),
            pltpu.VMEM((own_boxes, skel_rank, box_points), bf16),
            pltpu.VMEM((depth, box_points, box_points), bf16),
            pltpu.SMEM((max(chip_blocks, edge_blocks),), jnp.int32),
            pltpu.VMEM((own_boxes, 9, skel_rank, skel_rank), f32),
            pltpu.VMEM((skel_rank, box_points), bf16),
            pltpu.VMEM((skel_rank, box_points), bf16),
            pltpu.SemaphoreType.DMA((depth,)),
            pltpu.SemaphoreType.DMA((2 * own_boxes,)),
        ],
        compiler_params=params(20),
        cost_estimate=pl.CostEstimate(flops=8 * 10**9, bytes_accessed=32 * 10**6, transcendentals=0),
        name="chip_couple",
    )(core_arg, own_mask, chip_table, edge_table, basis, other_basis, store, edge_store)

    col, row, corner_a, corner_b, projected, give = lax.optimization_barrier(
        (col, row, corner_a, corner_b, projected, give)
    )
    second_col = swap(col)
    taken = swap(give)
    coupling, give = pl.pallas_call(
        edge_couple_kernel,
        out_shape=(coupling_shape, jax.ShapeDtypeStruct((edge_blocks, half_rank, skel_rank), f32)),
        in_specs=[SMEM] * 3 + [VMEM] + [ANY] * 7,
        out_specs=(ANY, VMEM),
        scratch_shapes=[
            pltpu.VMEM((edge_boxes, box_points, skel_rank), bf16),
            pltpu.VMEM((edge_blocks, skel_rank, skel_rank), f32),
            pltpu.SMEM((edge_blocks,), jnp.int32),
            pltpu.SemaphoreType.DMA((5,)),
            pltpu.SemaphoreType.DMA((edge_blocks,)),
            pltpu.SemaphoreType.DMA((own_boxes,)),
        ],
        input_output_aliases={10: 0},
        compiler_params=params(20),
        name="edge_couple",
    )(core_arg, own_mask, edge_table, projected, col, second_col, row, corner_a, corner_b, taken, coupling)
    taken = swap(give)
    coupling = pl.pallas_call(
        settle_kernel,
        out_shape=coupling_shape,
        in_specs=[SMEM] * 3 + [VMEM, ANY],
        out_specs=ANY,
        scratch_shapes=[pltpu.SemaphoreType.DMA((edge_blocks,))],
        input_output_aliases={4: 0},
        name="settle",
    )(core_arg, near_mask, edge_table, taken, coupling)
    basis_out = lax.dynamic_slice_in_dim(
        whole.reshape(chip_boxes, box_points, skel_rank), core * half_points, half_points, 1
    )
    return basis_out, coupling


def solution(mesh):
    return jax.shard_map(
        body,
        mesh=mesh,
        in_specs=(P("box", None, None), P("box", "col", None), P("box", None)),
        out_specs=(P("box", "col", None), P("box", None, "col", None)),
        check_vma=False,
    )
```

```python
import functools
import math

import jax
import jax.numpy as jnp
import numpy as np
from jax import lax
from jax.experimental import pallas as pl
from jax.experimental.pallas import tpu as pltpu
from jax.sharding import PartitionSpec as P

lift_scale = 0.25
LANES = 128
PANEL = 8
BLOCK = 32


def lane_copy(value, lane):
    return jnp.broadcast_to(value[:, lane:lane+1], value.shape)

def three_parts(value):
    first = value.astype(jnp.bfloat16)
    rest = value - first.astype(jnp.float32)
    second = rest.astype(jnp.bfloat16)
    third = (rest - second.astype(jnp.float32)).astype(jnp.bfloat16)
    return first, second, third

def factor_panel(rows, base):
    schur = [[lane_copy(rows[base + i], base + j) for j in range(i + 1)] for i in range(PANEL)]
    inverse_pivots, multipliers = [], [[None] * PANEL for _ in range(PANEL)]
    for k in range(PANEL):
        inverse_pivots.append(1.0 / schur[k][k])
        for i in range(k + 1, PANEL):
            multipliers[i][k] = schur[i][k] * inverse_pivots[k]
        for i in range(k + 1, PANEL):
            for j in range(k + 1, i + 1):
                schur[i][j] = schur[i][j] - multipliers[i][k] * schur[j][k]
    unit = [[None] * PANEL for _ in range(PANEL)]
    for i in range(PANEL):
        for j in range(i):
            total = multipliers[i][j]
            for t in range(j + 1, i):
                total = total + multipliers[i][t] * unit[t][j]
            unit[i][j] = -total
    return inverse_pivots, unit

def invert_factors(work, pivots, weights, exact):
    rank, batch, _ = work.shape
    lanes = lax.broadcasted_iota(jnp.int32, (batch, rank), 1)
    def turn_lanes(value, steps):
        return pltpu.roll(value, steps % rank, 1) if steps % rank else value

    for first in range(0, rank, BLOCK):
        rows = [turn_lanes(work[first + r], -first) for r in range(BLOCK)]
        for base in range(0, BLOCK, PANEL):
            inverse_pivots, unit = factor_panel(rows, base)
            inside = (lanes >= base) & (lanes < base + PANEL)
            held_rows, scaled_rows = [], []
            for k in range(PANEL):
                full = rows[base + k]
                for j in range(k):
                    full = full + unit[k][j] * rows[base + j]
                scaled = full * inverse_pivots[k]
                held = jnp.where(inside, 0.0, full)
                for j in range(k):
                    held = jnp.where(lanes == base + j, unit[k][j], held)
                held = jnp.where(lanes == base + k, 1.0, held)
                held_rows.append(held)
                scaled_rows.append(scaled)
            for t in range(base + PANEL, BLOCK):
                row = jnp.where(inside, 0.0, rows[t])
                for k in range(PANEL):
                    row = row - lane_copy(scaled_rows[k], t) * held_rows[k]
                rows[t] = row
            for k in range(PANEL):
                at = base + k
                kept = jnp.where((lanes > at) & (lanes < BLOCK), 0.0, held_rows[k])
                turned = turn_lanes(kept, first)
                pivots[at] = turned
                weights[at] = turn_lanes(scaled_rows[k], -BLOCK)
                work[first + at] = jnp.where(lanes <= first + at, turned, 0.0) * lax.sqrt(inverse_pivots[k])

        start = first + BLOCK
        left_over = rank - start
        if left_over == 0:
            continue
        inside = lax.broadcasted_iota(jnp.int32, (left_over, rank), 1)
        inside = (inside >= first) & (inside < start)
        for b in range(batch):
            a1, a2, a3 = three_parts(weights[:, b, :])
            b1, b2, b3 = three_parts(pivots[:, b, :])
            left = [a1, a1, a2] + ([a2, a1, a3] if exact else [])
            right = [b1, b2, b1] + ([b2, b3, b1] if exact else [])
            left, right = jnp.concatenate(left, axis=0)[:, :left_over], jnp.concatenate(right, axis=0)
            change = lax.dot_general(left, right, (((0,), (0,)), ((), ())), preferred_element_type=jnp.float32)
            work[start:, b, :] = jnp.where(inside, 0.0, work[start:, b, :]) - change


def two_part_product(left, right, dims):
    a1, a2, _ = three_parts(left)
    b1, b2, _ = three_parts(right)
    product = functools.partial(lax.dot_general, dimension_numbers=(dims, ((), ())), preferred_element_type=jnp.float32)
    return product(a1, b1) + (product(a1, b2) + product(a2, b1))


def whole_product(left, right, dims):
    return lax.dot_general(left, right, (dims, ((), ())), precision=lax.Precision.HIGHEST, preferred_element_type=jnp.float32)


def orthonormalize(y_ref, out_ref, work, pivots, weights):
    batch, points, rank = y_ref.shape
    for turn, product in enumerate((whole_product, two_part_product)):
        for b in range(batch):
            data = y_ref[b]
            work[:, b, :] = product(data, data, ((0,), (0,))) * (1.0 / points)
        invert_factors(work, pivots, weights, turn == 0)
        for b in range(batch):
            data = product(y_ref[b], work[:, b, :], ((1,), (1,)))
            if turn == 0:
                y_ref[b] = data
            else:
                out_ref[b] = data.astype(jnp.bfloat16)


def chip_entries(tile_side, rows_half, core):
    top = core * rows_half
    centres, pairs, singles = [], [], []
    for row in range(rows_half):
        for col in range(tile_side):
            own = row * tile_side + col
            for slot in range(9):
                offset_y, offset_x = slot // 3 - 1, slot % 3 - 1
                other_y, other_x = top + row + offset_y, col + offset_x
                if not (0 <= other_y < tile_side and 0 <= other_x < tile_side):
                    continue
                other = other_y * tile_side + other_x
                mate = other - top * tile_side
                entry = (own, other, offset_y, offset_x, slot, mate)
                if slot == 4:
                    centres.append(entry)
                elif top <= other_y < top + rows_half:
                    if slot > 4:
                        pairs.append(entry)
                else:
                    singles.append(entry[:5] + (-1,))
    return centres, pairs, singles


def edge_entries(tile_side, rows_half, core):
    top = core * rows_half
    corners = 3 * tile_side
    entries = []
    for row in range(rows_half):
        for col in range(tile_side):
            own = row * tile_side + col
            for slot in range(9):
                offset_y, offset_x = slot // 3 - 1, slot % 3 - 1
                other_y, other_x = top + row + offset_y, col + offset_x
                inside_y, inside_x = 0 <= other_y < tile_side, 0 <= other_x < tile_side
                if inside_y and inside_x:
                    continue
                if inside_x:
                    other = 2 * tile_side + other_x
                elif inside_y:
                    other = other_y + (tile_side if other_x > 0 else 0)
                else:
                    other = corners + (0 if (other_y > 0) == (other_x > 0) else 1)
                entries.append((own, other, offset_y, offset_x, slot, -1))
    return entries


def work_lists(tile_side, rows_half, cores):
    chip = [chip_entries(tile_side, rows_half, core) for core in range(cores)]
    edge = [edge_entries(tile_side, rows_half, core) for core in range(cores)]
    chip = [(centres + singles, pairs) for centres, pairs, singles in chip]
    counts = tuple(len(part) for part in chip[0])
    flat = [sum(parts, []) for parts in chip]
    return np.array(flat, np.int32), counts, np.array(edge, np.int32)


def fill_coords(coords, place, box_coords, stretch):
    moved = (box_coords - 0.5) * stretch
    coords[place] = jnp.zeros(coords.shape[1:], jnp.float32)
    coords[place, 0:2] = moved[0:2]
    coords[place, 2:3] = moved[2:3] * lift_scale


def fill_rows(rows, box_coords, own, soften):
    first = box_coords.astype(jnp.bfloat16).astype(jnp.float32)
    rest = box_coords - first
    second = rest.astype(jnp.bfloat16).astype(jnp.float32)
    parts = jnp.concatenate([first, second, rest - second], axis=0).astype(jnp.bfloat16)
    shape = (parts.shape[0], 3 * LANES)
    take = lax.rem(lax.broadcasted_iota(jnp.int32, shape, 0), 8) == lax.broadcasted_iota(jnp.int32, shape, 1) // LANES
    spread = lax.dot_general(
        parts,
        jnp.where(take, 1.0, 0.0).astype(jnp.bfloat16),
        (((0,), (0,)), ((), ())),
        preferred_element_type=jnp.float32,
    )
    total = soften
    for axis in range(3):
        column = spread[:, axis * LANES : (axis + 1) * LANES]
        rows[own, axis] = column + column
        total = total + column * column
    rows[own, 3] = total


def make_entries(target, rows, own, coords, other, shift_y, shift_x):
    box_points = coords.shape[2]
    step = 16
    columns = []
    for lane in range(0, box_points, LANES):
        here = pl.ds(lane, LANES)
        other_u = coords[other, 0:1, here] + shift_x
        other_v = coords[other, 1:2, here] + shift_y
        other_w = coords[other, 2:3, here]
        squares = other_u * other_u + other_v * other_v + other_w * other_w
        columns.append([jnp.broadcast_to(value, (step, LANES)) for value in (other_u, other_v, other_w, squares)])
    for first in range(0, box_points, step):
        part = slice(first, first + step)
        row_u, row_v, row_w, row_squares = (rows[own, axis, part, :] for axis in range(4))
        for strip, (other_u, other_v, other_w, squares) in enumerate(columns):
            apart = (row_squares + squares) - row_u * other_u - row_v * other_v - row_w * other_w
            target[part, strip * LANES : (strip + 1) * LANES] = lax.rsqrt(apart).astype(jnp.bfloat16)


def list_active(table, core, first, count, mask, active, base):
    def check(index, total):
        on = mask[table[core, first + index, 0], table[core, first + index, 4]] != 0

        @pl.when(on)
        def _():
            active[base + total] = first + index

        return total + jnp.where(on, 1, 0)

    return lax.fori_loop(0, count, check, 0)


def run_blocks(active, base, total, step_of):
    def step(turn, carry):
        step_of(active[base + turn])
        return carry

    lax.fori_loop(0, total, step, 0)


def place(table, core, index):
    return [table[core, index, field] for field in range(6)]


def chip_sketch_kernel(counts, core_ref, mask, table, points, mine, theirs, y_ref, store,
                       omega, omega_t, coords, rows, turned_y, blocks, active, load_sems, store_sems):
    core = core_ref[0]
    chip_boxes, _, box_points = points.shape
    own_boxes, _, skel_rank = y_ref.shape
    half = mine.shape[1]
    loads = [
        pltpu.make_async_copy(mine, omega.at[:, pl.ds(pl.multiple_of(core * half, half), half), :], load_sems.at[0]),
        pltpu.make_async_copy(theirs, omega.at[:, pl.ds(pl.multiple_of((1 - core) * half, half), half), :], load_sems.at[1]),
    ]
    for load in loads:
        load.start()
    stretch = math.sqrt(box_points) * 4.0
    soften = (0.25 / box_points) * stretch * stretch
    for box in range(chip_boxes):
        fill_coords(coords, box, points[box].astype(jnp.float32), stretch)
    for own in range(own_boxes):
        fill_rows(rows, coords[core * own_boxes + own], own, soften)
    for load in loads:
        load.wait()
    for own in range(own_boxes):
        values = omega[core * own_boxes + own]
        omega_t[own] = jnp.transpose(values)
        y_ref[own] = values.astype(jnp.float32)
        turned_y[own] = jnp.zeros((skel_rank, box_points), jnp.float32)

    def block(both, index):
        own, other, offset_y, offset_x, _, mate = place(table, core, index)
        shift_y, shift_x = offset_y.astype(jnp.float32) * stretch, offset_x.astype(jnp.float32) * stretch
        make_entries(blocks.at[index], rows, own, coords, other, shift_y, shift_x)
        send(index).start()
        values = blocks[index]
        y_ref[own] += jnp.dot(values, omega[other], preferred_element_type=jnp.float32)
        if both:
            turned_y[mate] += jnp.dot(omega_t[own], values, preferred_element_type=jnp.float32)

    def send(index):
        return pltpu.make_async_copy(blocks.at[index], store.at[index], store_sems.at[index])

    first, totals = 0, []
    for both, count in enumerate(counts):
        totals.append(list_active(table, core, first, count, mask, active, first))
        run_blocks(active, first, totals[both], functools.partial(block, both))
        first += count
    for own in range(own_boxes):
        y_ref[own] += jnp.transpose(turned_y[own])
    for first, total in zip((0, counts[0]), totals):
        run_blocks(active, first, total, lambda index: send(index).wait())


def edge_coords(coords, extended, box, box_points, stretch):
    packed = (extended[box, box_points : box_points + 16, :].astype(jnp.float32) - 0.5) * stretch
    strips = box_points // LANES
    for axis in range(3):
        for strip in range(strips):
            row = packed[axis * strips + strip : axis * strips + strip + 1, :]
            coords[box, axis : axis + 1, strip * LANES : (strip + 1) * LANES] = row * lift_scale if axis == 2 else row


def load_edges(core, pieces, extended, sems):
    first_col, second_col, row, corner_a, corner_b = pieces
    side = row.shape[0]
    return [
        pltpu.make_async_copy(first_col, extended.at[pl.ds(core * side, side)], sems.at[0]),
        pltpu.make_async_copy(second_col, extended.at[pl.ds((1 - core) * side, side)], sems.at[1]),
        pltpu.make_async_copy(row, extended.at[pl.ds(2 * side, side)], sems.at[2]),
        pltpu.make_async_copy(corner_a, extended.at[pl.ds(3 * side, 1)], sems.at[3]),
        pltpu.make_async_copy(corner_b, extended.at[pl.ds(3 * side + 1, 1)], sems.at[4]),
    ]


def edge_sketch_kernel(core_ref, mask, table, points, sketched, first_col, second_col, row, corner_a, corner_b,
                       basis, store, extended, coords, own_coords, rows, y_ref, blocks, active, filled, load_sems, store_sems,
                       work, pivots, weights):
    core = core_ref[0]
    own_boxes, box_points, skel_rank = y_ref.shape
    loads = load_edges(core, (first_col, second_col, row, corner_a, corner_b), extended, load_sems)
    loads.append(pltpu.make_async_copy(sketched, y_ref, load_sems.at[5]))
    for load in loads:
        load.start()
    stretch = math.sqrt(box_points) * 4.0
    soften = (0.25 / box_points) * stretch * stretch
    for own in range(own_boxes):
        fill_coords(own_coords, own, points[core * own_boxes + own].astype(jnp.float32), stretch)
    filled[0] = -1
    for load in loads:
        load.wait()
    for box in range(extended.shape[0]):
        edge_coords(coords, extended, box, box_points, stretch)

    def block(index):
        own, other, offset_y, offset_x, _, _ = place(table, core, index)
        shift_y, shift_x = offset_y.astype(jnp.float32) * stretch, offset_x.astype(jnp.float32) * stretch

        @pl.when(own != filled[0])
        def _():
            fill_rows(rows, own_coords[own], 0, soften)
            filled[0] = own

        make_entries(blocks.at[index], rows, 0, coords, other, shift_y, shift_x)
        send(index).start()
        y_ref[own] += jnp.dot(
            blocks[index], extended[other, 0:box_points, :], preferred_element_type=jnp.float32
        )

    def send(index):
        return pltpu.make_async_copy(blocks.at[index], store.at[index], store_sems.at[index])

    total = list_active(table, core, 0, table.shape[1], mask, active, 0)
    run_blocks(active, 0, total, block)
    orthonormalize(y_ref, basis, work, pivots, weights)
    run_blocks(active, 0, total, lambda index: send(index).wait())


def run_stored(active, base, total, fetch, project, use, pair):
    def entry(turn):
        return active[base + jnp.minimum(turn, total - 1)]

    @pl.when(total > 0)
    def _():
        fetch(entry(0)).wait()
        project(entry(0), pair[0])

    def step(half_turn, carry):
        even = 2 * half_turn
        for ahead in (0, 1):
            following = even + ahead + 1

            @pl.when(following < total)
            def _():
                fetch(entry(following)).wait()

            project(entry(following), pair[1 - ahead])
            use(entry(even + ahead), pair[ahead])
        return carry

    lax.fori_loop(0, (total + 1) // 2, step, 0)


def chip_couple_kernel(counts, core_ref, mask, table, edge_table, mine, theirs, store, edge_store,
                       full, give, projected, basis, basis_t, chip_held, blocks, active, edge_active, found, ray_a, ray_b, out_sems,
                       chip_sems, fetch_sems):
    core = core_ref[0]
    own_boxes, box_points, skel_rank = mine.shape

    def fetch(index):
        return pltpu.make_async_copy(edge_store.at[index], blocks.at[index], fetch_sems.at[index])

    def chip_fetch(index):
        return pltpu.make_async_copy(store.at[index], chip_held.at[index], chip_sems.at[index])

    first, totals = 0, []
    for count in counts:
        totals.append(list_active(table, core, first, count, mask, active, first))
        run_blocks(active, first, totals[-1], lambda index: chip_fetch(index).start())
        first += count
    edge_total = list_active(edge_table, core, 0, edge_table.shape[1], mask, edge_active, 0)
    run_blocks(edge_active, 0, edge_total, lambda index: fetch(index).start())
    half = give.shape[2]
    basis[pl.ds(core * own_boxes, own_boxes)] = mine[...]
    basis[pl.ds((1 - core) * own_boxes, own_boxes)] = theirs[...]
    for own in range(own_boxes):
        basis_t[own] = jnp.transpose(mine[own])

    def clear(index, carry):
        own, stencil = index // 9, lax.rem(index, 9)

        @pl.when(mask[own, stencil] == 0)
        def _():
            found[own, stencil] = jnp.zeros((skel_rank, skel_rank), jnp.float32)

        return carry

    lax.fori_loop(0, own_boxes * 9, clear, 0)

    def project(index, target):
        own, stencil = table[core, index, 0], table[core, index, 4]
        centre = jnp.where(stencil == 4, 1.0, 0.0)
        values = jnp.dot(basis_t[own], chip_held[index], preferred_element_type=jnp.float32)
        target[...] = (values + basis_t[own].astype(jnp.float32) * centre).astype(jnp.bfloat16)

    def use(both, index, rays):
        own, other, _, _, stencil, mate = place(table, core, index)
        values = jnp.dot(rays[...], basis[other], preferred_element_type=jnp.float32) * (1.0 / box_points)
        found[own, stencil] = values
        if both:
            found[mate, 8 - stencil] = jnp.transpose(values)

    first = 0
    for both, count in enumerate(counts):
        run_stored(active, first, totals[both], chip_fetch, project, functools.partial(use, both), (ray_a, ray_b))
        first += count

    copies = []
    for own in range(own_boxes):
        for side, (target, at) in enumerate(((full, core * own_boxes + own), (give, own))):
            rows_of = core if side == 0 else 1 - core
            copies.append(pltpu.make_async_copy(
                found.at[own, :, pl.ds(pl.multiple_of(rows_of * half, half), half), :],
                target.at[at],
                out_sems.at[2 * own + side],
            ))
    for copy in copies:
        copy.start()

    def edge_project(half_turn, carry):
        indices = []
        for turn in (2 * half_turn, 2 * half_turn + 1):
            indices.append(edge_active[jnp.minimum(turn, edge_total - 1)])

            @pl.when(turn < edge_total)
            def _():
                fetch(edge_active[turn]).wait()

        rays = [
            jnp.dot(basis_t[edge_table[core, index, 0]], blocks[index], preferred_element_type=jnp.float32)
            for index in indices
        ]
        for index, values in zip(indices, rays):
            projected[index] = values.astype(jnp.bfloat16)
        return carry

    lax.fori_loop(0, (edge_total + 1) // 2, edge_project, 0)
    for copy in copies:
        copy.wait()


def edge_couple_kernel(core_ref, mask, edge_table, projected, first_col, second_col, row, corner_a, corner_b,
                       full_in, full, give, extended, results, load_sems, sems):
    core = core_ref[0]
    box_points = projected.shape[2]
    own_boxes, half = full.shape[0] // 2, full.shape[2]
    loads = load_edges(core, (first_col, second_col, row, corner_a, corner_b), extended, load_sems)
    for copy in loads:
        copy.start()
    for load in loads:
        load.wait()
    copies = []
    for index in range(edge_table.shape[1]):
        own, other, stencil = (edge_table[core, index, field] for field in (0, 1, 4))
        values = jnp.dot(projected[index], extended[other], preferred_element_type=jnp.float32) * (1.0 / box_points)
        results[index] = jnp.where(mask[own, stencil] != 0, values, 0.0)
        copies.append(pltpu.make_async_copy(
            results.at[index, pl.ds(pl.multiple_of(core * half, half), half), :],
            full.at[core * own_boxes + own, stencil],
            sems.at[index],
        ))
    for index, copy in enumerate(copies):
        copy.start()
        give[index] = results[index, pl.ds(pl.multiple_of((1 - core) * half, half), half), :]
    for copy in copies:
        copy.wait()


def settle_kernel(core_ref, edge_table, bulk, taken, full_in, full, bulk_sems, sems):
    other = 1 - core_ref[0]
    own_boxes = full.shape[0] // 2
    moves = [
        pltpu.make_async_copy(bulk.at[own], full.at[other * own_boxes + own], bulk_sems.at[own])
        for own in range(own_boxes)
    ]
    for move in moves:
        move.start()
    for move in moves:
        move.wait()

    copies = [
        pltpu.make_async_copy(
            taken.at[index],
            full.at[other * own_boxes + edge_table[other, index, 0], edge_table[other, index, 4]],
            sems.at[index],
        )
        for index in range(edge_table.shape[1])
    ]
    for copy in copies:
        copy.start()
    for copy in copies:
        copy.wait()


SMEM = pl.BlockSpec(memory_space=pltpu.SMEM)
VMEM = pl.BlockSpec(memory_space=pltpu.VMEM)
ANY = pl.BlockSpec(memory_space=pl.ANY)
HBM = pl.BlockSpec(memory_space=pltpu.HBM)


def params(mebibytes):
    return pltpu.CompilerParams(vmem_limit_bytes=mebibytes << 20)


def exchange(boxes, core, grid_side):
    side = boxes.shape[0]

    def send(piece, step_y, step_x):
        pairs = []
        for tile in range(grid_side * grid_side):
            for member in range(2):
                sign = 2 * member - 1
                target_y, target_x = tile // grid_side + sign * step_y, tile % grid_side + sign * step_x
                if 0 <= target_y < grid_side and 0 <= target_x < grid_side:
                    target = target_y * grid_side + target_x
                    pairs.append((tile * 2 + member, target * 2 + 1 - member))
        return lax.ppermute(piece, ("box", "col"), pairs)

    last = side - 1
    low = core == 0
    col = send(jnp.where(low, boxes[:, 0], boxes[:, last]), 0, 1)
    row = send(jnp.where(low, boxes[0], boxes[last]), 1, 0)
    corner_a = send(jnp.where(low, boxes[0, 0:1], boxes[last, last:]), 1, 1)
    corner_b = send(jnp.where(low, boxes[0, last:], boxes[last, 0:1]), 1, -1)
    return col, row, corner_a, corner_b


def swap(value):
    return lax.ppermute(value, "col", [(0, 1), (1, 0)])


def body(points, sketch, near_mask):
    chip_boxes, _, box_points = points.shape
    half_points, skel_rank = sketch.shape[1:]
    tile_side = math.isqrt(chip_boxes)
    grid_side = math.isqrt(lax.axis_size("box"))
    cores = lax.axis_size("col")
    rows_half = tile_side // cores
    own_boxes = rows_half * tile_side
    half_rank = skel_rank // cores
    core = lax.axis_index("col")
    core_arg = core.astype(jnp.int32).reshape(1)
    chip_table, counts, edge_table = work_lists(tile_side, rows_half, cores)
    chip_blocks, edge_blocks = chip_table.shape[1], edge_table.shape[1]
    edge_boxes = 3 * tile_side + 2
    chip_table, edge_table = jnp.asarray(chip_table), jnp.asarray(edge_table)
    own_mask = lax.dynamic_slice_in_dim(near_mask, core * own_boxes, own_boxes, 0)
    low = core == 0

    theirs = swap(sketch)
    packed = points.reshape(chip_boxes, 3 * box_points // skel_rank, skel_rank)
    packed = jnp.pad(packed, ((0, 0), (0, 16 - packed.shape[1]), (0, 0)))
    whole = jnp.where(
        low,
        jnp.concatenate([sketch, theirs, packed], axis=1),
        jnp.concatenate([theirs, sketch, packed], axis=1),
    ).reshape(tile_side, tile_side, box_points + 16, skel_rank)
    col, row, corner_a, corner_b = exchange(whole, core, grid_side)

    bf16, f32 = jnp.bfloat16, jnp.float32
    sketched, store = pl.pallas_call(
        functools.partial(chip_sketch_kernel, counts),
        out_shape=(
            jax.ShapeDtypeStruct((own_boxes, box_points, skel_rank), f32),
            jax.ShapeDtypeStruct((chip_blocks, box_points, box_points), bf16),
        ),
        in_specs=[SMEM, SMEM, SMEM, VMEM, ANY, ANY],
        out_specs=(VMEM, HBM),
        scratch_shapes=[
            pltpu.VMEM((chip_boxes, box_points, skel_rank), bf16),
            pltpu.VMEM((own_boxes, skel_rank, box_points), bf16),
            pltpu.VMEM((chip_boxes, 8, box_points), f32),
            pltpu.VMEM((own_boxes, 4, box_points, LANES), f32),
            pltpu.VMEM((own_boxes, skel_rank, box_points), f32),
            pltpu.VMEM((chip_blocks, box_points, box_points), bf16),
            pltpu.SMEM((chip_blocks,), jnp.int32),
            pltpu.SemaphoreType.DMA((2,)),
            pltpu.SemaphoreType.DMA((chip_blocks,)),
        ],
        compiler_params=params(50),
        cost_estimate=pl.CostEstimate(flops=8 * 10**9, bytes_accessed=24 * 10**6, transcendentals=0),
        name="chip_sketch",
    )(core_arg, own_mask, chip_table, points, sketch, theirs)

    col, row, corner_a, corner_b, sketched = lax.optimization_barrier((col, row, corner_a, corner_b, sketched))
    second_col = swap(col)
    basis, edge_store = pl.pallas_call(
        edge_sketch_kernel,
        out_shape=(
            jax.ShapeDtypeStruct((own_boxes, box_points, skel_rank), bf16),
            jax.ShapeDtypeStruct((edge_blocks, box_points, box_points), bf16),
        ),
        in_specs=[SMEM, SMEM, SMEM, VMEM, ANY] + [ANY] * 5,
        out_specs=(VMEM, HBM),
        scratch_shapes=[
            pltpu.VMEM((edge_boxes, box_points + 16, skel_rank), bf16),
            pltpu.VMEM((edge_boxes, 8, box_points), f32),
            pltpu.VMEM((own_boxes, 8, box_points), f32),
            pltpu.VMEM((1, 4, box_points, LANES), f32),
            pltpu.VMEM((own_boxes, box_points, skel_rank), f32),
            pltpu.VMEM((edge_blocks, box_points, box_points), bf16),
            pltpu.SMEM((edge_blocks,), jnp.int32),
            pltpu.SMEM((1,), jnp.int32),
            pltpu.SemaphoreType.DMA((6,)),
            pltpu.SemaphoreType.DMA((edge_blocks,)),
            pltpu.VMEM((skel_rank, own_boxes, skel_rank), f32),
            pltpu.VMEM((BLOCK, own_boxes, skel_rank), f32),
            pltpu.VMEM((BLOCK, own_boxes, skel_rank), f32),
        ],
        compiler_params=params(50),
        name="edge_sketch",
    )(core_arg, own_mask, edge_table, points, sketched, col, second_col, row, corner_a, corner_b)

    other_basis = swap(basis)
    whole = jnp.where(
        low,
        jnp.concatenate([basis, other_basis], axis=0),
        jnp.concatenate([other_basis, basis], axis=0),
    ).reshape(tile_side, tile_side, box_points, skel_rank)
    col, row, corner_a, corner_b = exchange(whole, core, grid_side)
    coupling_shape = jax.ShapeDtypeStruct((chip_boxes, 9, half_rank, skel_rank), f32)
    coupling, give, projected = pl.pallas_call(
        functools.partial(chip_couple_kernel, counts),
        out_shape=(
            coupling_shape,
            jax.ShapeDtypeStruct((own_boxes, 9, half_rank, skel_rank), f32),
            jax.ShapeDtypeStruct((edge_blocks, skel_rank, box_points), bf16),
        ),
        in_specs=[SMEM] * 4 + [VMEM] * 2 + [HBM] * 2,
        out_specs=(ANY, ANY, VMEM),
        scratch_shapes=[
            pltpu.VMEM((chip_boxes, box_points, skel_rank), bf16),
            pltpu.VMEM((own_boxes, skel_rank, box_points), bf16),
            pltpu.VMEM((chip_blocks, box_points, box_points), bf16),
            pltpu.VMEM((edge_blocks, box_points, box_points), bf16),
            pltpu.SMEM((chip_blocks,), jnp.int32),
            pltpu.SMEM((edge_blocks,), jnp.int32),
            pltpu.VMEM((own_boxes, 9, skel_rank, skel_rank), f32),
            pltpu.VMEM((skel_rank, box_points), bf16),
            pltpu.VMEM((skel_rank, box_points), bf16),
            pltpu.SemaphoreType.DMA((2 * own_boxes,)),
            pltpu.SemaphoreType.DMA((chip_blocks,)),
            pltpu.SemaphoreType.DMA((edge_blocks,)),
        ],
        compiler_params=params(46),
        cost_estimate=pl.CostEstimate(flops=8 * 10**9, bytes_accessed=32 * 10**6, transcendentals=0),
        name="chip_couple",
    )(core_arg, own_mask, chip_table, edge_table, basis, other_basis, store, edge_store)

    col, row, corner_a, corner_b, projected, give = lax.optimization_barrier(
        (col, row, corner_a, corner_b, projected, give)
    )
    second_col, give = lax.optimization_barrier((swap(col), give))
    bulk = swap(give)
    coupling, give = pl.pallas_call(
        edge_couple_kernel,
        out_shape=(coupling_shape, jax.ShapeDtypeStruct((edge_blocks, half_rank, skel_rank), f32)),
        in_specs=[SMEM] * 3 + [VMEM] + [ANY] * 6,
        out_specs=(ANY, VMEM),
        scratch_shapes=[
            pltpu.VMEM((edge_boxes, box_points, skel_rank), bf16),
            pltpu.VMEM((edge_blocks, skel_rank, skel_rank), f32),
            pltpu.SemaphoreType.DMA((5,)),
            pltpu.SemaphoreType.DMA((edge_blocks,)),
        ],
        input_output_aliases={9: 0},
        compiler_params=params(20),
        name="edge_couple",
    )(core_arg, own_mask, edge_table, projected, col, second_col, row, corner_a, corner_b, coupling)
    taken = swap(give)
    coupling = pl.pallas_call(
        settle_kernel,
        out_shape=coupling_shape,
        in_specs=[SMEM] * 2 + [VMEM, VMEM, ANY],
        out_specs=ANY,
        scratch_shapes=[pltpu.SemaphoreType.DMA((own_boxes,)), pltpu.SemaphoreType.DMA((edge_blocks,))],
        input_output_aliases={4: 0},
        compiler_params=params(20),
        name="settle",
    )(core_arg, edge_table, bulk, taken, coupling)
    basis_out = lax.dynamic_slice_in_dim(
        whole.reshape(chip_boxes, box_points, skel_rank), core * half_points, half_points, 1
    )
    return basis_out, coupling


def solution(mesh):
    return jax.shard_map(
        body,
        mesh=mesh,
        in_specs=(P("box", None, None), P("box", "col", None), P("box", None)),
        out_specs=(P("box", "col", None), P("box", None, "col", None)),
        check_vma=False,
    )
```

```python
import functools
import math

import jax
import jax.numpy as jnp
import numpy as np
from jax import lax
from jax.experimental import pallas as pl
from jax.experimental.pallas import tpu as pltpu
from jax.sharding import PartitionSpec as P

lift_scale = 0.25
LANES = 128
PANEL = 8
BLOCK = 32


def lane_copy(value, lane):
    return jnp.broadcast_to(value[:, lane:lane+1], value.shape)

def three_parts(value):
    first = value.astype(jnp.bfloat16)
    rest = value - first.astype(jnp.float32)
    second = rest.astype(jnp.bfloat16)
    third = (rest - second.astype(jnp.float32)).astype(jnp.bfloat16)
    return first, second, third

def factor_panel(rows, base):
    schur = [[lane_copy(rows[base + i], base + j) for j in range(i + 1)] for i in range(PANEL)]
    inverse_pivots, multipliers = [], [[None] * PANEL for _ in range(PANEL)]
    for k in range(PANEL):
        inverse_pivots.append(1.0 / schur[k][k])
        for i in range(k + 1, PANEL):
            multipliers[i][k] = schur[i][k] * inverse_pivots[k]
        for i in range(k + 1, PANEL):
            for j in range(k + 1, i + 1):
                schur[i][j] = schur[i][j] - multipliers[i][k] * schur[j][k]
    unit = [[None] * PANEL for _ in range(PANEL)]
    for i in range(PANEL):
        for j in range(i):
            total = multipliers[i][j]
            for t in range(j + 1, i):
                total = total + multipliers[i][t] * unit[t][j]
            unit[i][j] = -total
    return inverse_pivots, unit

def invert_factors(work, pivots, weights, exact):
    rank, batch, _ = work.shape
    lanes = lax.broadcasted_iota(jnp.int32, (batch, rank), 1)
    def turn_lanes(value, steps):
        return pltpu.roll(value, steps % rank, 1) if steps % rank else value

    for first in range(0, rank, BLOCK):
        rows = [turn_lanes(work[first + r], -first) for r in range(BLOCK)]
        for base in range(0, BLOCK, PANEL):
            inverse_pivots, unit = factor_panel(rows, base)
            inside = (lanes >= base) & (lanes < base + PANEL)
            held_rows, scaled_rows = [], []
            for k in range(PANEL):
                full = rows[base + k]
                for j in range(k):
                    full = full + unit[k][j] * rows[base + j]
                scaled = full * inverse_pivots[k]
                held = jnp.where(inside, 0.0, full)
                for j in range(k):
                    held = jnp.where(lanes == base + j, unit[k][j], held)
                held = jnp.where(lanes == base + k, 1.0, held)
                held_rows.append(held)
                scaled_rows.append(scaled)
            for t in range(base + PANEL, BLOCK):
                row = jnp.where(inside, 0.0, rows[t])
                for k in range(PANEL):
                    row = row - lane_copy(scaled_rows[k], t) * held_rows[k]
                rows[t] = row
            for k in range(PANEL):
                at = base + k
                kept = jnp.where((lanes > at) & (lanes < BLOCK), 0.0, held_rows[k])
                turned = turn_lanes(kept, first)
                pivots[at] = turned
                weights[at] = turn_lanes(scaled_rows[k], -BLOCK)
                work[first + at] = jnp.where(lanes <= first + at, turned, 0.0) * lax.sqrt(inverse_pivots[k])

        start = first + BLOCK
        left_over = rank - start
        if left_over == 0:
            continue
        inside = lax.broadcasted_iota(jnp.int32, (left_over, rank), 1)
        inside = (inside >= first) & (inside < start)
        for b in range(batch):
            a1, a2, a3 = three_parts(weights[:, b, :])
            b1, b2, b3 = three_parts(pivots[:, b, :])
            left = [a1, a1, a2] + ([a2, a1, a3] if exact else [])
            right = [b1, b2, b1] + ([b2, b3, b1] if exact else [])
            left, right = jnp.concatenate(left, axis=0)[:, :left_over], jnp.concatenate(right, axis=0)
            change = lax.dot_general(left, right, (((0,), (0,)), ((), ())), preferred_element_type=jnp.float32)
            work[start:, b, :] = jnp.where(inside, 0.0, work[start:, b, :]) - change


def two_part_product(left, right, dims):
    a1, a2, _ = three_parts(left)
    b1, b2, _ = three_parts(right)
    product = functools.partial(lax.dot_general, dimension_numbers=(dims, ((), ())), preferred_element_type=jnp.float32)
    return product(a1, b1) + (product(a1, b2) + product(a2, b1))


def whole_product(left, right, dims):
    return lax.dot_general(left, right, (dims, ((), ())), precision=lax.Precision.HIGHEST, preferred_element_type=jnp.float32)


def orthonormalize(y_ref, out_ref, work, pivots, weights):
    batch, points, rank = y_ref.shape
    for turn, product in enumerate((whole_product, two_part_product)):
        for b in range(batch):
            data = y_ref[b]
            work[:, b, :] = product(data, data, ((0,), (0,))) * (1.0 / points)
        invert_factors(work, pivots, weights, turn == 0)
        for b in range(batch):
            data = product(y_ref[b], work[:, b, :], ((1,), (1,)))
            if turn == 0:
                y_ref[b] = data
            else:
                out_ref[b] = data.astype(jnp.bfloat16)


def chip_entries(tile_side, rows_half, core):
    top = core * rows_half
    centres, pairs, singles = [], [], []
    for row in range(rows_half):
        for col in range(tile_side):
            own = row * tile_side + col
            for slot in range(9):
                offset_y, offset_x = slot // 3 - 1, slot % 3 - 1
                other_y, other_x = top + row + offset_y, col + offset_x
                if not (0 <= other_y < tile_side and 0 <= other_x < tile_side):
                    continue
                other = other_y * tile_side + other_x
                mate = other - top * tile_side
                entry = (own, other, offset_y, offset_x, slot, mate)
                if slot == 4:
                    centres.append(entry)
                elif top <= other_y < top + rows_half:
                    if slot > 4:
                        pairs.append(entry)
                else:
                    singles.append(entry[:5] + (-1,))
    return centres, pairs, singles


def edge_entries(tile_side, rows_half, core):
    top = core * rows_half
    corners = 3 * tile_side
    entries = []
    for row in range(rows_half):
        for col in range(tile_side):
            own = row * tile_side + col
            for slot in range(9):
                offset_y, offset_x = slot // 3 - 1, slot % 3 - 1
                other_y, other_x = top + row + offset_y, col + offset_x
                inside_y, inside_x = 0 <= other_y < tile_side, 0 <= other_x < tile_side
                if inside_y and inside_x:
                    continue
                if inside_x:
                    other = 2 * tile_side + other_x
                elif inside_y:
                    other = other_y + (tile_side if other_x > 0 else 0)
                else:
                    other = corners + (0 if (other_y > 0) == (other_x > 0) else 1)
                entries.append((own, other, offset_y, offset_x, slot, -1))
    return entries


def work_lists(tile_side, rows_half, cores):
    chip = [chip_entries(tile_side, rows_half, core) for core in range(cores)]
    edge = [edge_entries(tile_side, rows_half, core) for core in range(cores)]
    chip = [(centres + singles, pairs) for centres, pairs, singles in chip]
    counts = tuple(len(part) for part in chip[0])
    flat = [sum(parts, []) for parts in chip]
    return np.array(flat, np.int32), counts, np.array(edge, np.int32)


def fill_coords(coords, place, box_coords, stretch):
    moved = (box_coords - 0.5) * stretch
    coords[place] = jnp.zeros(coords.shape[1:], jnp.float32)
    coords[place, 0:2] = moved[0:2]
    coords[place, 2:3] = moved[2:3] * lift_scale


def fill_rows(rows, box_coords, own, soften):
    first = box_coords.astype(jnp.bfloat16).astype(jnp.float32)
    rest = box_coords - first
    second = rest.astype(jnp.bfloat16).astype(jnp.float32)
    parts = jnp.concatenate([first, second, rest - second], axis=0).astype(jnp.bfloat16)
    shape = (parts.shape[0], 3 * LANES)
    take = lax.rem(lax.broadcasted_iota(jnp.int32, shape, 0), 8) == lax.broadcasted_iota(jnp.int32, shape, 1) // LANES
    spread = lax.dot_general(
        parts,
        jnp.where(take, 1.0, 0.0).astype(jnp.bfloat16),
        (((0,), (0,)), ((), ())),
        preferred_element_type=jnp.float32,
    )
    total = soften
    for axis in range(3):
        column = spread[:, axis * LANES : (axis + 1) * LANES]
        rows[own, axis] = column + column
        total = total + column * column
    rows[own, 3] = total


def make_entries(target, rows, own, coords, other, shift_y, shift_x):
    box_points = coords.shape[2]
    step = 16
    columns = []
    for lane in range(0, box_points, LANES):
        here = pl.ds(lane, LANES)
        other_u = coords[other, 0:1, here] + shift_x
        other_v = coords[other, 1:2, here] + shift_y
        other_w = coords[other, 2:3, here]
        squares = other_u * other_u + other_v * other_v + other_w * other_w
        columns.append([jnp.broadcast_to(value, (step, LANES)) for value in (other_u, other_v, other_w, squares)])
    for first in range(0, box_points, step):
        part = slice(first, first + step)
        row_u, row_v, row_w, row_squares = (rows[own, axis, part, :] for axis in range(4))
        for strip, (other_u, other_v, other_w, squares) in enumerate(columns):
            apart = (row_squares + squares) - row_u * other_u - row_v * other_v - row_w * other_w
            target[part, strip * LANES : (strip + 1) * LANES] = lax.rsqrt(apart).astype(jnp.bfloat16)


def list_active(table, core, first, count, mask, active, base):
    def check(index, total):
        on = mask[table[core, first + index, 0], table[core, first + index, 4]] != 0

        @pl.when(on)
        def _():
            active[base + total] = first + index

        return total + jnp.where(on, 1, 0)

    return lax.fori_loop(0, count, check, 0)


def run_blocks(active, base, total, step_of):
    def step(turn, carry):
        step_of(active[base + turn])
        return carry

    lax.fori_loop(0, total, step, 0)


def place(table, core, index):
    return [table[core, index, field] for field in range(6)]


def chip_sketch_kernel(counts, core_ref, mask, table, points, mine, theirs, y_ref, store,
                       omega, omega_t, coords, rows, turned_y, blocks, active, load_sems, store_sems):
    core = core_ref[0]
    chip_boxes, _, box_points = points.shape
    own_boxes, _, skel_rank = y_ref.shape
    half = mine.shape[1]
    loads = [
        pltpu.make_async_copy(mine, omega.at[:, pl.ds(pl.multiple_of(core * half, half), half), :], load_sems.at[0]),
        pltpu.make_async_copy(theirs, omega.at[:, pl.ds(pl.multiple_of((1 - core) * half, half), half), :], load_sems.at[1]),
    ]
    for load in loads:
        load.start()
    stretch = math.sqrt(box_points) * 4.0
    soften = (0.25 / box_points) * stretch * stretch
    for box in range(chip_boxes):
        fill_coords(coords, box, points[box].astype(jnp.float32), stretch)
    for own in range(own_boxes):
        fill_rows(rows, coords[core * own_boxes + own], own, soften)
    for load in loads:
        load.wait()
    for own in range(own_boxes):
        values = omega[core * own_boxes + own]
        omega_t[own] = jnp.transpose(values)
        y_ref[own] = values.astype(jnp.float32)
        turned_y[own] = jnp.zeros((skel_rank, box_points), jnp.float32)

    def block(both, index):
        own, other, offset_y, offset_x, _, mate = place(table, core, index)
        shift_y, shift_x = offset_y.astype(jnp.float32) * stretch, offset_x.astype(jnp.float32) * stretch
        make_entries(blocks.at[index], rows, own, coords, other, shift_y, shift_x)
        send(index).start()
        values = blocks[index]
        y_ref[own] += jnp.dot(values, omega[other], preferred_element_type=jnp.float32)
        if both:
            turned_y[mate] += jnp.dot(omega_t[own], values, preferred_element_type=jnp.float32)

    def send(index):
        return pltpu.make_async_copy(blocks.at[index], store.at[index], store_sems.at[index])

    first, totals = 0, []
    for both, count in enumerate(counts):
        totals.append(list_active(table, core, first, count, mask, active, first))
        run_blocks(active, first, totals[both], functools.partial(block, both))
        first += count
    for own in range(own_boxes):
        y_ref[own] += jnp.transpose(turned_y[own])
    for first, total in zip((0, counts[0]), totals):
        run_blocks(active, first, total, lambda index: send(index).wait())


def edge_coords(coords, extended, box, box_points, stretch):
    packed = (extended[box, box_points : box_points + 16, :].astype(jnp.float32) - 0.5) * stretch
    strips = box_points // LANES
    for axis in range(3):
        for strip in range(strips):
            row = packed[axis * strips + strip : axis * strips + strip + 1, :]
            coords[box, axis : axis + 1, strip * LANES : (strip + 1) * LANES] = row * lift_scale if axis == 2 else row


def load_edges(core, pieces, extended, sems):
    first_col, second_col, row, corner_a, corner_b = pieces
    side = row.shape[0]
    return [
        pltpu.make_async_copy(first_col, extended.at[pl.ds(core * side, side)], sems.at[0]),
        pltpu.make_async_copy(second_col, extended.at[pl.ds((1 - core) * side, side)], sems.at[1]),
        pltpu.make_async_copy(row, extended.at[pl.ds(2 * side, side)], sems.at[2]),
        pltpu.make_async_copy(corner_a, extended.at[pl.ds(3 * side, 1)], sems.at[3]),
        pltpu.make_async_copy(corner_b, extended.at[pl.ds(3 * side + 1, 1)], sems.at[4]),
    ]


def edge_sketch_kernel(core_ref, mask, table, points, sketched, first_col, second_col, row, corner_a, corner_b,
                       basis, store, extended, coords, own_coords, rows, y_ref, blocks, active, filled, load_sems, store_sems,
                       work, pivots, weights):
    core = core_ref[0]
    own_boxes, box_points, skel_rank = y_ref.shape
    loads = load_edges(core, (first_col, second_col, row, corner_a, corner_b), extended, load_sems)
    loads.append(pltpu.make_async_copy(sketched, y_ref, load_sems.at[5]))
    for load in loads:
        load.start()
    stretch = math.sqrt(box_points) * 4.0
    soften = (0.25 / box_points) * stretch * stretch
    for own in range(own_boxes):
        fill_coords(own_coords, own, points[core * own_boxes + own].astype(jnp.float32), stretch)
    filled[0] = -1
    for load in loads:
        load.wait()
    for box in range(extended.shape[0]):
        edge_coords(coords, extended, box, box_points, stretch)

    def block(index):
        own, other, offset_y, offset_x, _, _ = place(table, core, index)
        shift_y, shift_x = offset_y.astype(jnp.float32) * stretch, offset_x.astype(jnp.float32) * stretch

        @pl.when(own != filled[0])
        def _():
            fill_rows(rows, own_coords[own], 0, soften)
            filled[0] = own

        make_entries(blocks.at[index], rows, 0, coords, other, shift_y, shift_x)
        send(index).start()
        y_ref[own] += jnp.dot(
            blocks[index], extended[other, 0:box_points, :], preferred_element_type=jnp.float32
        )

    def send(index):
        return pltpu.make_async_copy(blocks.at[index], store.at[index], store_sems.at[index])

    total = list_active(table, core, 0, table.shape[1], mask, active, 0)
    run_blocks(active, 0, total, block)
    orthonormalize(y_ref, basis, work, pivots, weights)
    run_blocks(active, 0, total, lambda index: send(index).wait())


def run_stored(active, base, total, fetch, project, use, pair):
    def entry(turn):
        return active[base + jnp.minimum(turn, total - 1)]

    @pl.when(total > 0)
    def _():
        fetch(entry(0)).wait()
        project(entry(0), pair[0])

    def step(half_turn, carry):
        even = 2 * half_turn
        for ahead in (0, 1):
            following = even + ahead + 1

            @pl.when(following < total)
            def _():
                fetch(entry(following)).wait()

            project(entry(following), pair[1 - ahead])
            use(entry(even + ahead), pair[ahead])
        return carry

    lax.fori_loop(0, (total + 1) // 2, step, 0)


def chip_couple_kernel(counts, core_ref, mask, table, edge_table, mine, theirs, store, edge_store,
                       full, give, projected, basis_out, basis, basis_t, chip_held, blocks, active, edge_active, found, ray_a, ray_b, out_sems,
                       chip_sems, fetch_sems, basis_sem):
    core = core_ref[0]
    own_boxes, box_points, skel_rank = mine.shape

    def fetch(index):
        return pltpu.make_async_copy(edge_store.at[index], blocks.at[index], fetch_sems.at[index])

    def chip_fetch(index):
        return pltpu.make_async_copy(store.at[index], chip_held.at[index], chip_sems.at[index])

    first, totals = 0, []
    for count in counts:
        totals.append(list_active(table, core, first, count, mask, active, first))
        run_blocks(active, first, totals[-1], lambda index: chip_fetch(index).start())
        first += count
    edge_total = list_active(edge_table, core, 0, edge_table.shape[1], mask, edge_active, 0)
    run_blocks(edge_active, 0, edge_total, lambda index: fetch(index).start())
    half = give.shape[2]
    basis[pl.ds(core * own_boxes, own_boxes)] = mine[...]
    basis[pl.ds((1 - core) * own_boxes, own_boxes)] = theirs[...]
    half_points = box_points // 2
    basis_copy = pltpu.make_async_copy(
        basis.at[:, pl.ds(pl.multiple_of(core * half_points, half_points), half_points), :], basis_out, basis_sem.at[0]
    )
    basis_copy.start()
    for own in range(own_boxes):
        basis_t[own] = jnp.transpose(mine[own])

    def clear(index, carry):
        own, stencil = index // 9, lax.rem(index, 9)

        @pl.when(mask[own, stencil] == 0)
        def _():
            found[own, stencil] = jnp.zeros((skel_rank, skel_rank), jnp.float32)

        return carry

    lax.fori_loop(0, own_boxes * 9, clear, 0)

    def project(index, target):
        own, stencil = table[core, index, 0], table[core, index, 4]
        centre = jnp.where(stencil == 4, 1.0, 0.0)
        values = jnp.dot(basis_t[own], chip_held[index], preferred_element_type=jnp.float32)
        target[...] = (values + basis_t[own].astype(jnp.float32) * centre).astype(jnp.bfloat16)

    def use(both, index, rays):
        own, other, _, _, stencil, mate = place(table, core, index)
        values = jnp.dot(rays[...], basis[other], preferred_element_type=jnp.float32) * (1.0 / box_points)
        found[own, stencil] = values
        if both:
            found[mate, 8 - stencil] = jnp.transpose(values)

    first = 0
    for both, count in enumerate(counts):
        run_stored(active, first, totals[both], chip_fetch, project, functools.partial(use, both), (ray_a, ray_b))
        first += count

    copies = []
    for own in range(own_boxes):
        for side, (target, at) in enumerate(((full, core * own_boxes + own), (give, own))):
            rows_of = core if side == 0 else 1 - core
            copies.append(pltpu.make_async_copy(
                found.at[own, :, pl.ds(pl.multiple_of(rows_of * half, half), half), :],
                target.at[at],
                out_sems.at[2 * own + side],
            ))
    for copy in copies:
        copy.start()

    def edge_project(half_turn, carry):
        indices = []
        for turn in (2 * half_turn, 2 * half_turn + 1):
            indices.append(edge_active[jnp.minimum(turn, edge_total - 1)])

            @pl.when(turn < edge_total)
            def _():
                fetch(edge_active[turn]).wait()

        rays = [
            jnp.dot(basis_t[edge_table[core, index, 0]], blocks[index], preferred_element_type=jnp.float32)
            for index in indices
        ]
        for index, values in zip(indices, rays):
            projected[index] = values.astype(jnp.bfloat16)
        return carry

    lax.fori_loop(0, (edge_total + 1) // 2, edge_project, 0)
    basis_copy.wait()
    for copy in copies:
        copy.wait()


def edge_couple_kernel(core_ref, mask, edge_table, projected, first_col, second_col, row, corner_a, corner_b,
                       full_in, full, give, extended, results, load_sems, sems):
    core = core_ref[0]
    box_points = projected.shape[2]
    own_boxes, half = full.shape[0] // 2, full.shape[2]
    loads = load_edges(core, (first_col, second_col, row, corner_a, corner_b), extended, load_sems)
    for copy in loads:
        copy.start()
    for load in loads:
        load.wait()
    copies = []
    for index in range(edge_table.shape[1]):
        own, other, stencil = (edge_table[core, index, field] for field in (0, 1, 4))
        values = jnp.dot(projected[index], extended[other], preferred_element_type=jnp.float32) * (1.0 / box_points)
        results[index] = jnp.where(mask[own, stencil] != 0, values, 0.0)
        copies.append(pltpu.make_async_copy(
            results.at[index, pl.ds(pl.multiple_of(core * half, half), half), :],
            full.at[core * own_boxes + own, stencil],
            sems.at[index],
        ))
    for index, copy in enumerate(copies):
        copy.start()
        give[index] = results[index, pl.ds(pl.multiple_of((1 - core) * half, half), half), :]
    for copy in copies:
        copy.wait()


def bulk_kernel(core_ref, bulk, full_in, full, sems):
    other = 1 - core_ref[0]
    own_boxes = full.shape[0] // 2
    copies = [
        pltpu.make_async_copy(bulk.at[own], full.at[other * own_boxes + own], sems.at[own])
        for own in range(own_boxes)
    ]
    for copy in copies:
        copy.start()
    for copy in copies:
        copy.wait()


def settle_kernel(core_ref, edge_table, taken, full_in, full, sems):
    other = 1 - core_ref[0]
    own_boxes = full.shape[0] // 2
    copies = [
        pltpu.make_async_copy(
            taken.at[index],
            full.at[other * own_boxes + edge_table[other, index, 0], edge_table[other, index, 4]],
            sems.at[index],
        )
        for index in range(edge_table.shape[1])
    ]
    for copy in copies:
        copy.start()
    for copy in copies:
        copy.wait()


SMEM = pl.BlockSpec(memory_space=pltpu.SMEM)
VMEM = pl.BlockSpec(memory_space=pltpu.VMEM)
ANY = pl.BlockSpec(memory_space=pl.ANY)
HBM = pl.BlockSpec(memory_space=pltpu.HBM)


def params(mebibytes):
    return pltpu.CompilerParams(vmem_limit_bytes=mebibytes << 20)


def exchange(parts, join, core, grid_side):
    side = parts[0].shape[0]

    def send(piece, step_y, step_x):
        pairs = []
        for tile in range(grid_side * grid_side):
            for member in range(2):
                sign = 2 * member - 1
                target_y, target_x = tile // grid_side + sign * step_y, tile % grid_side + sign * step_x
                if 0 <= target_y < grid_side and 0 <= target_x < grid_side:
                    target = target_y * grid_side + target_x
                    pairs.append((tile * 2 + member, target * 2 + 1 - member))
        return lax.ppermute(piece, ("box", "col"), pairs)

    last = side - 1
    low = core == 0

    def border(below, above):
        return join(*(jnp.where(low, part[below], part[above]) for part in parts))

    every = slice(None)
    col = send(border((every, 0), (every, last)), 0, 1)
    row = send(border((0,), (last,)), 1, 0)
    corner_a = send(border((0, slice(0, 1)), (last, slice(last, side))), 1, 1)
    corner_b = send(border((0, slice(last, side)), (last, slice(0, 1))), 1, -1)
    return col, row, corner_a, corner_b


def swap(value):
    return lax.ppermute(value, "col", [(0, 1), (1, 0)])


def body(points, sketch, near_mask):
    chip_boxes, _, box_points = points.shape
    half_points, skel_rank = sketch.shape[1:]
    tile_side = math.isqrt(chip_boxes)
    grid_side = math.isqrt(lax.axis_size("box"))
    cores = lax.axis_size("col")
    rows_half = tile_side // cores
    own_boxes = rows_half * tile_side
    half_rank = skel_rank // cores
    core = lax.axis_index("col")
    core_arg = core.astype(jnp.int32).reshape(1)
    chip_table, counts, edge_table = work_lists(tile_side, rows_half, cores)
    chip_blocks, edge_blocks = chip_table.shape[1], edge_table.shape[1]
    edge_boxes = 3 * tile_side + 2
    chip_table, edge_table = jnp.asarray(chip_table), jnp.asarray(edge_table)
    own_mask = lax.dynamic_slice_in_dim(near_mask, core * own_boxes, own_boxes, 0)
    low = core == 0

    theirs = swap(sketch)
    packed = points.reshape(chip_boxes, 3 * box_points // skel_rank, skel_rank)
    packed = jnp.pad(packed, ((0, 0), (0, 16 - packed.shape[1]), (0, 0)))

    def join(mine, other, coords):
        return jnp.where(
            low,
            jnp.concatenate([mine, other, coords], axis=1),
            jnp.concatenate([other, mine, coords], axis=1),
        )

    parts = [part.reshape((tile_side, tile_side) + part.shape[1:]) for part in (sketch, theirs, packed)]
    col, row, corner_a, corner_b = exchange(parts, join, core, grid_side)

    bf16, f32 = jnp.bfloat16, jnp.float32
    sketched, store = pl.pallas_call(
        functools.partial(chip_sketch_kernel, counts),
        out_shape=(
            jax.ShapeDtypeStruct((own_boxes, box_points, skel_rank), f32),
            jax.ShapeDtypeStruct((chip_blocks, box_points, box_points), bf16),
        ),
        in_specs=[SMEM, SMEM, SMEM, VMEM, ANY, ANY],
        out_specs=(VMEM, HBM),
        scratch_shapes=[
            pltpu.VMEM((chip_boxes, box_points, skel_rank), bf16),
            pltpu.VMEM((own_boxes, skel_rank, box_points), bf16),
            pltpu.VMEM((chip_boxes, 8, box_points), f32),
            pltpu.VMEM((own_boxes, 4, box_points, LANES), f32),
            pltpu.VMEM((own_boxes, skel_rank, box_points), f32),
            pltpu.VMEM((chip_blocks, box_points, box_points), bf16),
            pltpu.SMEM((chip_blocks,), jnp.int32),
            pltpu.SemaphoreType.DMA((2,)),
            pltpu.SemaphoreType.DMA((chip_blocks,)),
        ],
        compiler_params=params(50),
        cost_estimate=pl.CostEstimate(flops=8 * 10**9, bytes_accessed=24 * 10**6, transcendentals=0),
        name="chip_sketch",
    )(core_arg, own_mask, chip_table, points, sketch, theirs)

    col, row, corner_a, corner_b, sketched = lax.optimization_barrier((col, row, corner_a, corner_b, sketched))
    second_col = swap(col)
    basis, edge_store = pl.pallas_call(
        edge_sketch_kernel,
        out_shape=(
            jax.ShapeDtypeStruct((own_boxes, box_points, skel_rank), bf16),
            jax.ShapeDtypeStruct((edge_blocks, box_points, box_points), bf16),
        ),
        in_specs=[SMEM, SMEM, SMEM, VMEM, ANY] + [ANY] * 5,
        out_specs=(VMEM, HBM),
        scratch_shapes=[
            pltpu.VMEM((edge_boxes, box_points + 16, skel_rank), bf16),
            pltpu.VMEM((edge_boxes, 8, box_points), f32),
            pltpu.VMEM((own_boxes, 8, box_points), f32),
            pltpu.VMEM((1, 4, box_points, LANES), f32),
            pltpu.VMEM((own_boxes, box_points, skel_rank), f32),
            pltpu.VMEM((edge_blocks, box_points, box_points), bf16),
            pltpu.SMEM((edge_blocks,), jnp.int32),
            pltpu.SMEM((1,), jnp.int32),
            pltpu.SemaphoreType.DMA((6,)),
            pltpu.SemaphoreType.DMA((edge_blocks,)),
            pltpu.VMEM((skel_rank, own_boxes, skel_rank), f32),
            pltpu.VMEM((BLOCK, own_boxes, skel_rank), f32),
            pltpu.VMEM((BLOCK, own_boxes, skel_rank), f32),
        ],
        compiler_params=params(50),
        name="edge_sketch",
    )(core_arg, own_mask, edge_table, points, sketched, col, second_col, row, corner_a, corner_b)

    other_basis = swap(basis)
    whole = jnp.where(
        low,
        jnp.concatenate([basis, other_basis], axis=0),
        jnp.concatenate([other_basis, basis], axis=0),
    ).reshape(tile_side, tile_side, box_points, skel_rank)
    col, row, corner_a, corner_b = exchange([whole], lambda boxes: boxes, core, grid_side)
    coupling_shape = jax.ShapeDtypeStruct((chip_boxes, 9, half_rank, skel_rank), f32)
    coupling, give, projected, basis_out = pl.pallas_call(
        functools.partial(chip_couple_kernel, counts),
        out_shape=(
            coupling_shape,
            jax.ShapeDtypeStruct((own_boxes, 9, half_rank, skel_rank), f32),
            jax.ShapeDtypeStruct((edge_blocks, skel_rank, box_points), bf16),
            jax.ShapeDtypeStruct((chip_boxes, half_points, skel_rank), bf16),
        ),
        in_specs=[SMEM] * 4 + [VMEM] * 2 + [HBM] * 2,
        out_specs=(ANY, ANY, VMEM, ANY),
        scratch_shapes=[
            pltpu.VMEM((chip_boxes, box_points, skel_rank), bf16),
            pltpu.VMEM((own_boxes, skel_rank, box_points), bf16),
            pltpu.VMEM((chip_blocks, box_points, box_points), bf16),
            pltpu.VMEM((edge_blocks, box_points, box_points), bf16),
            pltpu.SMEM((chip_blocks,), jnp.int32),
            pltpu.SMEM((edge_blocks,), jnp.int32),
            pltpu.VMEM((own_boxes, 9, skel_rank, skel_rank), f32),
            pltpu.VMEM((skel_rank, box_points), bf16),
            pltpu.VMEM((skel_rank, box_points), bf16),
            pltpu.SemaphoreType.DMA((2 * own_boxes,)),
            pltpu.SemaphoreType.DMA((chip_blocks,)),
            pltpu.SemaphoreType.DMA((edge_blocks,)),
            pltpu.SemaphoreType.DMA((1,)),
        ],
        compiler_params=params(46),
        cost_estimate=pl.CostEstimate(flops=8 * 10**9, bytes_accessed=32 * 10**6, transcendentals=0),
        name="chip_couple",
    )(core_arg, own_mask, chip_table, edge_table, basis, other_basis, store, edge_store)

    col, row, corner_a, corner_b, projected, give = lax.optimization_barrier(
        (col, row, corner_a, corner_b, projected, give)
    )
    second_col, give = lax.optimization_barrier((swap(col), give))
    bulk = swap(give)
    coupling, give = pl.pallas_call(
        edge_couple_kernel,
        out_shape=(coupling_shape, jax.ShapeDtypeStruct((edge_blocks, half_rank, skel_rank), f32)),
        in_specs=[SMEM] * 3 + [VMEM] + [ANY] * 6,
        out_specs=(ANY, VMEM),
        scratch_shapes=[
            pltpu.VMEM((edge_boxes, box_points, skel_rank), bf16),
            pltpu.VMEM((edge_blocks, skel_rank, skel_rank), f32),
            pltpu.SemaphoreType.DMA((5,)),
            pltpu.SemaphoreType.DMA((edge_blocks,)),
        ],
        input_output_aliases={9: 0},
        compiler_params=params(20),
        name="edge_couple",
    )(core_arg, own_mask, edge_table, projected, col, second_col, row, corner_a, corner_b, coupling)
    taken = swap(give)
    coupling = pl.pallas_call(
        bulk_kernel,
        out_shape=coupling_shape,
        in_specs=[SMEM, VMEM, ANY],
        out_specs=ANY,
        scratch_shapes=[pltpu.SemaphoreType.DMA((own_boxes,))],
        input_output_aliases={2: 0},
        compiler_params=params(12),
        cost_estimate=pl.CostEstimate(flops=0, bytes_accessed=10 * 10**6, transcendentals=0),
        name="bulk",
    )(core_arg, bulk, coupling)
    coupling = pl.pallas_call(
        settle_kernel,
        out_shape=coupling_shape,
        in_specs=[SMEM] * 2 + [VMEM, ANY],
        out_specs=ANY,
        scratch_shapes=[pltpu.SemaphoreType.DMA((edge_blocks,))],
        input_output_aliases={3: 0},
        compiler_params=params(12),
        name="settle",
    )(core_arg, edge_table, taken, coupling)
    return basis_out, coupling


def solution(mesh):
    return jax.shard_map(
        body,
        mesh=mesh,
        in_specs=(P("box", None, None), P("box", "col", None), P("box", None)),
        out_specs=(P("box", "col", None), P("box", None, "col", None)),
        check_vma=False,
    )
```

```python
import functools
import math

import jax
import jax.numpy as jnp
import numpy as np
from jax import lax
from jax.experimental import pallas as pl
from jax.experimental.pallas import tpu as pltpu
from jax.sharding import PartitionSpec as P

lift_scale = 0.25
LANES = 128
PANEL = 8
BLOCK = 32


def lane_copy(value, lane):
    return jnp.broadcast_to(value[:, lane:lane+1], value.shape)

def three_parts(value):
    first = value.astype(jnp.bfloat16)
    rest = value - first.astype(jnp.float32)
    second = rest.astype(jnp.bfloat16)
    third = (rest - second.astype(jnp.float32)).astype(jnp.bfloat16)
    return first, second, third

def factor_panel(rows, base):
    schur = [[lane_copy(rows[base + i], base + j) for j in range(i + 1)] for i in range(PANEL)]
    inverse_pivots, multipliers = [], [[None] * PANEL for _ in range(PANEL)]
    for k in range(PANEL):
        inverse_pivots.append(1.0 / schur[k][k])
        for i in range(k + 1, PANEL):
            multipliers[i][k] = schur[i][k] * inverse_pivots[k]
        for i in range(k + 1, PANEL):
            for j in range(k + 1, i + 1):
                schur[i][j] = schur[i][j] - multipliers[i][k] * schur[j][k]
    unit = [[None] * PANEL for _ in range(PANEL)]
    for i in range(PANEL):
        for j in range(i):
            total = multipliers[i][j]
            for t in range(j + 1, i):
                total = total + multipliers[i][t] * unit[t][j]
            unit[i][j] = -total
    return inverse_pivots, unit

def invert_factors(work, pivots, weights, exact):
    rank, batch, _ = work.shape
    lanes = lax.broadcasted_iota(jnp.int32, (batch, rank), 1)
    def turn_lanes(value, steps):
        return pltpu.roll(value, steps % rank, 1) if steps % rank else value

    for first in range(0, rank, BLOCK):
        rows = [turn_lanes(work[first + r], -first) for r in range(BLOCK)]
        for base in range(0, BLOCK, PANEL):
            inverse_pivots, unit = factor_panel(rows, base)
            inside = (lanes >= base) & (lanes < base + PANEL)
            held_rows, scaled_rows = [], []
            for k in range(PANEL):
                full = rows[base + k]
                for j in range(k):
                    full = full + unit[k][j] * rows[base + j]
                scaled = full * inverse_pivots[k]
                held = jnp.where(inside, 0.0, full)
                for j in range(k):
                    held = jnp.where(lanes == base + j, unit[k][j], held)
                held = jnp.where(lanes == base + k, 1.0, held)
                held_rows.append(held)
                scaled_rows.append(scaled)
            for t in range(base + PANEL, BLOCK):
                row = jnp.where(inside, 0.0, rows[t])
                for k in range(PANEL):
                    row = row - lane_copy(scaled_rows[k], t) * held_rows[k]
                rows[t] = row
            for k in range(PANEL):
                at = base + k
                kept = jnp.where((lanes > at) & (lanes < BLOCK), 0.0, held_rows[k])
                turned = turn_lanes(kept, first)
                pivots[at] = turned
                weights[at] = turn_lanes(scaled_rows[k], -BLOCK)
                work[first + at] = jnp.where(lanes <= first + at, turned, 0.0) * lax.sqrt(inverse_pivots[k])

        start = first + BLOCK
        left_over = rank - start
        if left_over == 0:
            continue
        inside = lax.broadcasted_iota(jnp.int32, (left_over, rank), 1)
        inside = (inside >= first) & (inside < start)
        for b in range(batch):
            a1, a2, a3 = three_parts(weights[:, b, :])
            b1, b2, b3 = three_parts(pivots[:, b, :])
            left = [a1, a1, a2] + ([a2, a1, a3] if exact else [])
            right = [b1, b2, b1] + ([b2, b3, b1] if exact else [])
            left, right = jnp.concatenate(left, axis=0)[:, :left_over], jnp.concatenate(right, axis=0)
            change = lax.dot_general(left, right, (((0,), (0,)), ((), ())), preferred_element_type=jnp.float32)
            work[start:, b, :] = jnp.where(inside, 0.0, work[start:, b, :]) - change


def two_part_product(left, right, dims):
    a1, a2, _ = three_parts(left)
    b1, b2, _ = three_parts(right)
    product = functools.partial(lax.dot_general, dimension_numbers=(dims, ((), ())), preferred_element_type=jnp.float32)
    return product(a1, b1) + (product(a1, b2) + product(a2, b1))


def whole_product(left, right, dims):
    return lax.dot_general(left, right, (dims, ((), ())), precision=lax.Precision.HIGHEST, preferred_element_type=jnp.float32)


def orthonormalize(y_ref, out_ref, work, pivots, weights):
    batch, points, rank = y_ref.shape
    for turn, product in enumerate((whole_product, two_part_product)):
        for b in range(batch):
            data = y_ref[b]
            work[:, b, :] = product(data, data, ((0,), (0,))) * (1.0 / points)
        invert_factors(work, pivots, weights, turn == 0)
        for b in range(batch):
            data = product(y_ref[b], work[:, b, :], ((1,), (1,)))
            if turn == 0:
                y_ref[b] = data
            else:
                out_ref[b] = data.astype(jnp.bfloat16)


def chip_entries(tile_side, rows_half, core):
    top = core * rows_half
    centres, pairs, singles = [], [], []
    for row in range(rows_half):
        for col in range(tile_side):
            own = row * tile_side + col
            for slot in range(9):
                offset_y, offset_x = slot // 3 - 1, slot % 3 - 1
                other_y, other_x = top + row + offset_y, col + offset_x
                if not (0 <= other_y < tile_side and 0 <= other_x < tile_side):
                    continue
                other = other_y * tile_side + other_x
                mate = other - top * tile_side
                entry = (own, other, offset_y, offset_x, slot, mate)
                if slot == 4:
                    centres.append(entry)
                elif top <= other_y < top + rows_half:
                    if slot > 4:
                        pairs.append(entry)
                else:
                    singles.append(entry[:5] + (-1,))
    return centres, pairs, singles


def edge_entries(tile_side, rows_half, core):
    top = core * rows_half
    corners = 3 * tile_side
    entries = []
    for row in range(rows_half):
        for col in range(tile_side):
            own = row * tile_side + col
            for slot in range(9):
                offset_y, offset_x = slot // 3 - 1, slot % 3 - 1
                other_y, other_x = top + row + offset_y, col + offset_x
                inside_y, inside_x = 0 <= other_y < tile_side, 0 <= other_x < tile_side
                if inside_y and inside_x:
                    continue
                if inside_x:
                    other = 2 * tile_side + other_x
                elif inside_y:
                    other = other_y + (tile_side if other_x > 0 else 0)
                else:
                    other = corners + (0 if (other_y > 0) == (other_x > 0) else 1)
                entries.append((own, other, offset_y, offset_x, slot, -1))
    return entries


def work_lists(tile_side, rows_half, cores):
    chip = [chip_entries(tile_side, rows_half, core) for core in range(cores)]
    edge = [edge_entries(tile_side, rows_half, core) for core in range(cores)]
    chip = [(centres + singles, pairs) for centres, pairs, singles in chip]
    counts = tuple(len(part) for part in chip[0])
    flat = [sum(parts, []) for parts in chip]
    return np.array(flat, np.int32), counts, np.array(edge, np.int32)


def fill_coords(coords, place, box_coords, stretch):
    moved = (box_coords - 0.5) * stretch
    coords[place] = jnp.zeros(coords.shape[1:], jnp.float32)
    coords[place, 0:2] = moved[0:2]
    coords[place, 2:3] = moved[2:3] * lift_scale


def fill_rows(rows, box_coords, own, soften):
    first = box_coords.astype(jnp.bfloat16).astype(jnp.float32)
    rest = box_coords - first
    second = rest.astype(jnp.bfloat16).astype(jnp.float32)
    parts = jnp.concatenate([first, second, rest - second], axis=0).astype(jnp.bfloat16)
    shape = (parts.shape[0], 3 * LANES)
    take = lax.rem(lax.broadcasted_iota(jnp.int32, shape, 0), 8) == lax.broadcasted_iota(jnp.int32, shape, 1) // LANES
    spread = lax.dot_general(
        parts,
        jnp.where(take, 1.0, 0.0).astype(jnp.bfloat16),
        (((0,), (0,)), ((), ())),
        preferred_element_type=jnp.float32,
    )
    total = soften
    for axis in range(3):
        column = spread[:, axis * LANES : (axis + 1) * LANES]
        rows[own, axis] = column + column
        total = total + column * column
    rows[own, 3] = total


def make_entries(target, rows, own, coords, other, shift_y, shift_x):
    box_points = coords.shape[2]
    step = 16
    columns = []
    for lane in range(0, box_points, LANES):
        here = pl.ds(lane, LANES)
        other_u = coords[other, 0:1, here] + shift_x
        other_v = coords[other, 1:2, here] + shift_y
        other_w = coords[other, 2:3, here]
        squares = other_u * other_u + other_v * other_v + other_w * other_w
        columns.append([jnp.broadcast_to(value, (step, LANES)) for value in (other_u, other_v, other_w, squares)])
    for first in range(0, box_points, step):
        part = slice(first, first + step)
        row_u, row_v, row_w, row_squares = (rows[own, axis, part, :] for axis in range(4))
        for strip, (other_u, other_v, other_w, squares) in enumerate(columns):
            apart = (row_squares + squares) - row_u * other_u - row_v * other_v - row_w * other_w
            target[part, strip * LANES : (strip + 1) * LANES] = lax.rsqrt(apart).astype(jnp.bfloat16)


def list_active(table, core, first, count, mask, active, base):
    def check(index, total):
        on = mask[table[core, first + index, 0], table[core, first + index, 4]] != 0

        @pl.when(on)
        def _():
            active[base + total] = first + index

        return total + jnp.where(on, 1, 0)

    return lax.fori_loop(0, count, check, 0)


def run_blocks(active, base, total, step_of):
    def step(turn, carry):
        step_of(active[base + turn])
        return carry

    lax.fori_loop(0, total, step, 0)


def place(table, core, index):
    return [table[core, index, field] for field in range(6)]


def chip_sketch_kernel(counts, core_ref, mask, table, points, mine, theirs, y_ref, store,
                       omega, omega_t, coords, rows, turned_y, blocks, active, load_sems, store_sems):
    core = core_ref[0]
    chip_boxes, _, box_points = points.shape
    own_boxes, _, skel_rank = y_ref.shape
    half = mine.shape[1]
    loads = [
        pltpu.make_async_copy(mine, omega.at[:, pl.ds(pl.multiple_of(core * half, half), half), :], load_sems.at[0]),
        pltpu.make_async_copy(theirs, omega.at[:, pl.ds(pl.multiple_of((1 - core) * half, half), half), :], load_sems.at[1]),
    ]
    for load in loads:
        load.start()
    stretch = math.sqrt(box_points) * 4.0
    soften = (0.25 / box_points) * stretch * stretch
    for box in range(chip_boxes):
        fill_coords(coords, box, points[box].astype(jnp.float32), stretch)
    for own in range(own_boxes):
        fill_rows(rows, coords[core * own_boxes + own], own, soften)
    for load in loads:
        load.wait()
    for own in range(own_boxes):
        values = omega[core * own_boxes + own]
        omega_t[own] = jnp.transpose(values)
        y_ref[own] = values.astype(jnp.float32)
        turned_y[own] = jnp.zeros((skel_rank, box_points), jnp.float32)

    def block(both, index):
        own, other, offset_y, offset_x, _, mate = place(table, core, index)
        shift_y, shift_x = offset_y.astype(jnp.float32) * stretch, offset_x.astype(jnp.float32) * stretch
        make_entries(blocks.at[index], rows, own, coords, other, shift_y, shift_x)
        send(index).start()
        values = blocks[index]
        y_ref[own] += jnp.dot(values, omega[other], preferred_element_type=jnp.float32)
        if both:
            turned_y[mate] += jnp.dot(omega_t[own], values, preferred_element_type=jnp.float32)

    def send(index):
        return pltpu.make_async_copy(blocks.at[index], store.at[index], store_sems.at[index])

    first, totals = 0, []
    for both, count in enumerate(counts):
        totals.append(list_active(table, core, first, count, mask, active, first))
        run_blocks(active, first, totals[both], functools.partial(block, both))
        first += count
    for own in range(own_boxes):
        y_ref[own] += jnp.transpose(turned_y[own])
    for first, total in zip((0, counts[0]), totals):
        run_blocks(active, first, total, lambda index: send(index).wait())


def edge_coords(coords, extended, box, box_points, stretch):
    packed = (extended[box, box_points : box_points + 16, :].astype(jnp.float32) - 0.5) * stretch
    strips = box_points // LANES
    for axis in range(3):
        for strip in range(strips):
            row = packed[axis * strips + strip : axis * strips + strip + 1, :]
            coords[box, axis : axis + 1, strip * LANES : (strip + 1) * LANES] = row * lift_scale if axis == 2 else row


def load_edges(core, pieces, extended, sems):
    first_col, second_col, row, corner_a, corner_b = pieces
    side = row.shape[0]
    return [
        pltpu.make_async_copy(first_col, extended.at[pl.ds(core * side, side)], sems.at[0]),
        pltpu.make_async_copy(second_col, extended.at[pl.ds((1 - core) * side, side)], sems.at[1]),
        pltpu.make_async_copy(row, extended.at[pl.ds(2 * side, side)], sems.at[2]),
        pltpu.make_async_copy(corner_a, extended.at[pl.ds(3 * side, 1)], sems.at[3]),
        pltpu.make_async_copy(corner_b, extended.at[pl.ds(3 * side + 1, 1)], sems.at[4]),
    ]


def edge_sketch_kernel(core_ref, mask, table, points, sketched, first_col, second_col, row, corner_a, corner_b,
                       basis, store, extended, coords, own_coords, rows, y_ref, blocks, active, load_sems, store_sems,
                       work, pivots, weights):
    core = core_ref[0]
    own_boxes, box_points, skel_rank = y_ref.shape
    loads = load_edges(core, (first_col, second_col, row, corner_a, corner_b), extended, load_sems)
    loads.append(pltpu.make_async_copy(sketched, y_ref, load_sems.at[5]))
    for load in loads:
        load.start()
    stretch = math.sqrt(box_points) * 4.0
    soften = (0.25 / box_points) * stretch * stretch
    for own in range(own_boxes):
        fill_coords(own_coords, own, points[core * own_boxes + own].astype(jnp.float32), stretch)
        fill_rows(rows, own_coords[own], own, soften)
    for load in loads:
        load.wait()
    for box in range(extended.shape[0]):
        edge_coords(coords, extended, box, box_points, stretch)

    def block(index):
        own, other, offset_y, offset_x, _, _ = place(table, core, index)
        shift_y, shift_x = offset_y.astype(jnp.float32) * stretch, offset_x.astype(jnp.float32) * stretch

        make_entries(blocks.at[index], rows, own, coords, other, shift_y, shift_x)
        send(index).start()
        y_ref[own] += jnp.dot(
            blocks[index], extended[other, 0:box_points, :], preferred_element_type=jnp.float32
        )

    def send(index):
        return pltpu.make_async_copy(blocks.at[index], store.at[index], store_sems.at[index])

    total = list_active(table, core, 0, table.shape[1], mask, active, 0)
    run_blocks(active, 0, total, block)
    orthonormalize(y_ref, basis, work, pivots, weights)
    run_blocks(active, 0, total, lambda index: send(index).wait())


def run_stored(active, base, total, fetch, project, use, pair):
    def entry(turn):
        return active[base + jnp.minimum(turn, total - 1)]

    @pl.when(total > 0)
    def _():
        fetch(entry(0)).wait()
        project(entry(0), pair[0])

    def step(half_turn, carry):
        even = 2 * half_turn
        for ahead in (0, 1):
            following = even + ahead + 1

            @pl.when(following < total)
            def _():
                fetch(entry(following)).wait()

            project(entry(following), pair[1 - ahead])
            use(entry(even + ahead), pair[ahead])
        return carry

    lax.fori_loop(0, (total + 1) // 2, step, 0)


def chip_couple_kernel(counts, core_ref, mask, table, edge_table, mine, theirs, store, edge_store,
                       full, give, projected, basis_out, basis, basis_t, chip_held, blocks, active, edge_active, found, ray_a, ray_b, out_sems,
                       chip_sems, fetch_sems, basis_sem):
    core = core_ref[0]
    own_boxes, box_points, skel_rank = mine.shape

    def fetch(index):
        return pltpu.make_async_copy(edge_store.at[index], blocks.at[index], fetch_sems.at[index])

    def chip_fetch(index):
        return pltpu.make_async_copy(store.at[index], chip_held.at[index], chip_sems.at[index])

    first, totals = 0, []
    for count in counts:
        totals.append(list_active(table, core, first, count, mask, active, first))
        run_blocks(active, first, totals[-1], lambda index: chip_fetch(index).start())
        first += count
    edge_total = list_active(edge_table, core, 0, edge_table.shape[1], mask, edge_active, 0)
    run_blocks(edge_active, 0, edge_total, lambda index: fetch(index).start())
    half = give.shape[2]
    basis[pl.ds(core * own_boxes, own_boxes)] = mine[...]
    basis[pl.ds((1 - core) * own_boxes, own_boxes)] = theirs[...]
    half_points = box_points // 2
    basis_copy = pltpu.make_async_copy(
        basis.at[:, pl.ds(pl.multiple_of(core * half_points, half_points), half_points), :], basis_out, basis_sem.at[0]
    )
    basis_copy.start()
    for own in range(own_boxes):
        basis_t[own] = jnp.transpose(mine[own])

    def clear(index, carry):
        own, stencil = index // 9, lax.rem(index, 9)

        @pl.when(mask[own, stencil] == 0)
        def _():
            found[own, stencil] = jnp.zeros((skel_rank, skel_rank), jnp.float32)

        return carry

    lax.fori_loop(0, own_boxes * 9, clear, 0)

    def project(index, target):
        own, stencil = table[core, index, 0], table[core, index, 4]
        centre = jnp.where(stencil == 4, 1.0, 0.0)
        values = jnp.dot(basis_t[own], chip_held[index], preferred_element_type=jnp.float32)
        target[...] = (values + basis_t[own].astype(jnp.float32) * centre).astype(jnp.bfloat16)

    def use(both, index, rays):
        own, other, _, _, stencil, mate = place(table, core, index)
        values = jnp.dot(rays[...], basis[other], preferred_element_type=jnp.float32) * (1.0 / box_points)
        found[own, stencil] = values
        if both:
            found[mate, 8 - stencil] = jnp.transpose(values)

    first = 0
    for both, count in enumerate(counts):
        run_stored(active, first, totals[both], chip_fetch, project, functools.partial(use, both), (ray_a, ray_b))
        first += count

    copies = []
    for own in range(own_boxes):
        for side, (target, at) in enumerate(((full, core * own_boxes + own), (give, own))):
            rows_of = core if side == 0 else 1 - core
            copies.append(pltpu.make_async_copy(
                found.at[own, :, pl.ds(pl.multiple_of(rows_of * half, half), half), :],
                target.at[at],
                out_sems.at[2 * own + side],
            ))
    for copy in copies:
        copy.start()

    def edge_project(half_turn, carry):
        indices = []
        for turn in (2 * half_turn, 2 * half_turn + 1):
            indices.append(edge_active[jnp.minimum(turn, edge_total - 1)])

            @pl.when(turn < edge_total)
            def _():
                fetch(edge_active[turn]).wait()

        rays = [
            jnp.dot(basis_t[edge_table[core, index, 0]], blocks[index], preferred_element_type=jnp.float32)
            for index in indices
        ]
        for index, values in zip(indices, rays):
            projected[index] = values.astype(jnp.bfloat16)
        return carry

    lax.fori_loop(0, (edge_total + 1) // 2, edge_project, 0)
    basis_copy.wait()
    for copy in copies:
        copy.wait()


def edge_couple_kernel(core_ref, mask, edge_table, projected, first_col, second_col, row, corner_a, corner_b,
                       full_in, full, give, extended, results, load_sems, sems):
    core = core_ref[0]
    box_points = projected.shape[2]
    own_boxes, half = full.shape[0] // 2, full.shape[2]
    loads = load_edges(core, (first_col, second_col, row, corner_a, corner_b), extended, load_sems)
    for copy in loads:
        copy.start()
    for load in loads:
        load.wait()
    copies = []
    for index in range(edge_table.shape[1]):
        own, other, stencil = (edge_table[core, index, field] for field in (0, 1, 4))
        values = jnp.dot(projected[index], extended[other], preferred_element_type=jnp.float32) * (1.0 / box_points)
        results[index] = jnp.where(mask[own, stencil] != 0, values, 0.0)
        copies.append(pltpu.make_async_copy(
            results.at[index, pl.ds(pl.multiple_of(core * half, half), half), :],
            full.at[core * own_boxes + own, stencil],
            sems.at[index],
        ))
    for index, copy in enumerate(copies):
        copy.start()
        give[index] = results[index, pl.ds(pl.multiple_of((1 - core) * half, half), half), :]
    for copy in copies:
        copy.wait()


def bulk_kernel(core_ref, bulk, full_in, full, sems):
    other = 1 - core_ref[0]
    own_boxes = full.shape[0] // 2
    copies = [
        pltpu.make_async_copy(bulk.at[own], full.at[other * own_boxes + own], sems.at[own])
        for own in range(own_boxes)
    ]
    for copy in copies:
        copy.start()
    for copy in copies:
        copy.wait()


def settle_kernel(core_ref, edge_table, taken, full_in, full, sems):
    other = 1 - core_ref[0]
    own_boxes = full.shape[0] // 2
    copies = [
        pltpu.make_async_copy(
            taken.at[index],
            full.at[other * own_boxes + edge_table[other, index, 0], edge_table[other, index, 4]],
            sems.at[index],
        )
        for index in range(edge_table.shape[1])
    ]
    for copy in copies:
        copy.start()
    for copy in copies:
        copy.wait()


SMEM = pl.BlockSpec(memory_space=pltpu.SMEM)
VMEM = pl.BlockSpec(memory_space=pltpu.VMEM)
ANY = pl.BlockSpec(memory_space=pl.ANY)
HBM = pl.BlockSpec(memory_space=pltpu.HBM)


def params(mebibytes):
    return pltpu.CompilerParams(vmem_limit_bytes=mebibytes << 20)


def exchange(parts, join, core, grid_side):
    side = parts[0].shape[0]

    def send(piece, step_y, step_x):
        pairs = []
        for tile in range(grid_side * grid_side):
            for member in range(2):
                sign = 2 * member - 1
                target_y, target_x = tile // grid_side + sign * step_y, tile % grid_side + sign * step_x
                if 0 <= target_y < grid_side and 0 <= target_x < grid_side:
                    target = target_y * grid_side + target_x
                    pairs.append((tile * 2 + member, target * 2 + 1 - member))
        return lax.ppermute(piece, ("box", "col"), pairs)

    last = side - 1
    low = core == 0

    def border(below, above):
        return join(*(jnp.where(low, part[below], part[above]) for part in parts))

    every = slice(None)
    col = send(border((every, 0), (every, last)), 0, 1)
    row = send(border((0,), (last,)), 1, 0)
    corner_a = send(border((0, slice(0, 1)), (last, slice(last, side))), 1, 1)
    corner_b = send(border((0, slice(last, side)), (last, slice(0, 1))), 1, -1)
    return col, row, corner_a, corner_b


def swap(value):
    return lax.ppermute(value, "col", [(0, 1), (1, 0)])


def body(points, sketch, near_mask):
    chip_boxes, _, box_points = points.shape
    half_points, skel_rank = sketch.shape[1:]
    tile_side = math.isqrt(chip_boxes)
    grid_side = math.isqrt(lax.axis_size("box"))
    cores = lax.axis_size("col")
    rows_half = tile_side // cores
    own_boxes = rows_half * tile_side
    half_rank = skel_rank // cores
    core = lax.axis_index("col")
    core_arg = core.astype(jnp.int32).reshape(1)
    chip_table, counts, edge_table = work_lists(tile_side, rows_half, cores)
    chip_blocks, edge_blocks = chip_table.shape[1], edge_table.shape[1]
    edge_boxes = 3 * tile_side + 2
    chip_table, edge_table = jnp.asarray(chip_table), jnp.asarray(edge_table)
    own_mask = lax.dynamic_slice_in_dim(near_mask, core * own_boxes, own_boxes, 0)
    low = core == 0

    theirs = swap(sketch)
    packed = points.reshape(chip_boxes, 3 * box_points // skel_rank, skel_rank)
    packed = jnp.pad(packed, ((0, 0), (0, 16 - packed.shape[1]), (0, 0)))

    def join(mine, other, coords):
        return jnp.where(
            low,
            jnp.concatenate([mine, other, coords], axis=1),
            jnp.concatenate([other, mine, coords], axis=1),
        )

    parts = [part.reshape((tile_side, tile_side) + part.shape[1:]) for part in (sketch, theirs, packed)]
    col, row, corner_a, corner_b = exchange(parts, join, core, grid_side)

    bf16, f32 = jnp.bfloat16, jnp.float32
    sketched, store = pl.pallas_call(
        functools.partial(chip_sketch_kernel, counts),
        out_shape=(
            jax.ShapeDtypeStruct((own_boxes, box_points, skel_rank), f32),
            jax.ShapeDtypeStruct((chip_blocks, box_points, box_points), bf16),
        ),
        in_specs=[SMEM, SMEM, SMEM, VMEM, ANY, ANY],
        out_specs=(VMEM, HBM),
        scratch_shapes=[
            pltpu.VMEM((chip_boxes, box_points, skel_rank), bf16),
            pltpu.VMEM((own_boxes, skel_rank, box_points), bf16),
            pltpu.VMEM((chip_boxes, 8, box_points), f32),
            pltpu.VMEM((own_boxes, 4, box_points, LANES), f32),
            pltpu.VMEM((own_boxes, skel_rank, box_points), f32),
            pltpu.VMEM((chip_blocks, box_points, box_points), bf16),
            pltpu.SMEM((chip_blocks,), jnp.int32),
            pltpu.SemaphoreType.DMA((2,)),
            pltpu.SemaphoreType.DMA((chip_blocks,)),
        ],
        compiler_params=params(50),
        cost_estimate=pl.CostEstimate(flops=8 * 10**9, bytes_accessed=24 * 10**6, transcendentals=0),
        name="chip_sketch",
    )(core_arg, own_mask, chip_table, points, sketch, theirs)

    col, row, corner_a, corner_b, sketched = lax.optimization_barrier((col, row, corner_a, corner_b, sketched))
    second_col = swap(col)
    basis, edge_store = pl.pallas_call(
        edge_sketch_kernel,
        out_shape=(
            jax.ShapeDtypeStruct((own_boxes, box_points, skel_rank), bf16),
            jax.ShapeDtypeStruct((edge_blocks, box_points, box_points), bf16),
        ),
        in_specs=[SMEM, SMEM, SMEM, VMEM, ANY] + [ANY] * 5,
        out_specs=(VMEM, HBM),
        scratch_shapes=[
            pltpu.VMEM((edge_boxes, box_points + 16, skel_rank), bf16),
            pltpu.VMEM((edge_boxes, 8, box_points), f32),
            pltpu.VMEM((own_boxes, 8, box_points), f32),
            pltpu.VMEM((own_boxes, 4, box_points, LANES), f32),
            pltpu.VMEM((own_boxes, box_points, skel_rank), f32),
            pltpu.VMEM((edge_blocks, box_points, box_points), bf16),
            pltpu.SMEM((edge_blocks,), jnp.int32),
            pltpu.SemaphoreType.DMA((6,)),
            pltpu.SemaphoreType.DMA((edge_blocks,)),
            pltpu.VMEM((skel_rank, own_boxes, skel_rank), f32),
            pltpu.VMEM((BLOCK, own_boxes, skel_rank), f32),
            pltpu.VMEM((BLOCK, own_boxes, skel_rank), f32),
        ],
        compiler_params=params(50),
        name="edge_sketch",
    )(core_arg, own_mask, edge_table, points, sketched, col, second_col, row, corner_a, corner_b)

    other_basis = swap(basis)
    whole = jnp.where(
        low,
        jnp.concatenate([basis, other_basis], axis=0),
        jnp.concatenate([other_basis, basis], axis=0),
    ).reshape(tile_side, tile_side, box_points, skel_rank)
    col, row, corner_a, corner_b = exchange([whole], lambda boxes: boxes, core, grid_side)
    coupling_shape = jax.ShapeDtypeStruct((chip_boxes, 9, half_rank, skel_rank), f32)
    coupling, give, projected, basis_out = pl.pallas_call(
        functools.partial(chip_couple_kernel, counts),
        out_shape=(
            coupling_shape,
            jax.ShapeDtypeStruct((own_boxes, 9, half_rank, skel_rank), f32),
            jax.ShapeDtypeStruct((edge_blocks, skel_rank, box_points), bf16),
            jax.ShapeDtypeStruct((chip_boxes, half_points, skel_rank), bf16),
        ),
        in_specs=[SMEM] * 4 + [VMEM] * 2 + [HBM] * 2,
        out_specs=(ANY, ANY, VMEM, ANY),
        scratch_shapes=[
            pltpu.VMEM((chip_boxes, box_points, skel_rank), bf16),
            pltpu.VMEM((own_boxes, skel_rank, box_points), bf16),
            pltpu.VMEM((chip_blocks, box_points, box_points), bf16),
            pltpu.VMEM((edge_blocks, box_points, box_points), bf16),
            pltpu.SMEM((chip_blocks,), jnp.int32),
            pltpu.SMEM((edge_blocks,), jnp.int32),
            pltpu.VMEM((own_boxes, 9, skel_rank, skel_rank), f32),
            pltpu.VMEM((skel_rank, box_points), bf16),
            pltpu.VMEM((skel_rank, box_points), bf16),
            pltpu.SemaphoreType.DMA((2 * own_boxes,)),
            pltpu.SemaphoreType.DMA((chip_blocks,)),
            pltpu.SemaphoreType.DMA((edge_blocks,)),
            pltpu.SemaphoreType.DMA((1,)),
        ],
        compiler_params=params(46),
        cost_estimate=pl.CostEstimate(flops=8 * 10**9, bytes_accessed=32 * 10**6, transcendentals=0),
        name="chip_couple",
    )(core_arg, own_mask, chip_table, edge_table, basis, other_basis, store, edge_store)

    col, row, corner_a, corner_b, projected, give = lax.optimization_barrier(
        (col, row, corner_a, corner_b, projected, give)
    )
    second_col, give = lax.optimization_barrier((swap(col), give))
    bulk = swap(give)
    coupling, give = pl.pallas_call(
        edge_couple_kernel,
        out_shape=(coupling_shape, jax.ShapeDtypeStruct((edge_blocks, half_rank, skel_rank), f32)),
        in_specs=[SMEM] * 3 + [VMEM] + [ANY] * 6,
        out_specs=(ANY, VMEM),
        scratch_shapes=[
            pltpu.VMEM((edge_boxes, box_points, skel_rank), bf16),
            pltpu.VMEM((edge_blocks, skel_rank, skel_rank), f32),
            pltpu.SemaphoreType.DMA((5,)),
            pltpu.SemaphoreType.DMA((edge_blocks,)),
        ],
        input_output_aliases={9: 0},
        compiler_params=params(20),
        name="edge_couple",
    )(core_arg, own_mask, edge_table, projected, col, second_col, row, corner_a, corner_b, coupling)
    taken = swap(give)
    coupling = pl.pallas_call(
        bulk_kernel,
        out_shape=coupling_shape,
        in_specs=[SMEM, VMEM, ANY],
        out_specs=ANY,
        scratch_shapes=[pltpu.SemaphoreType.DMA((own_boxes,))],
        input_output_aliases={2: 0},
        compiler_params=params(12),
        cost_estimate=pl.CostEstimate(flops=0, bytes_accessed=10 * 10**6, transcendentals=0),
        name="bulk",
    )(core_arg, bulk, coupling)
    coupling = pl.pallas_call(
        settle_kernel,
        out_shape=coupling_shape,
        in_specs=[SMEM] * 2 + [VMEM, ANY],
        out_specs=ANY,
        scratch_shapes=[pltpu.SemaphoreType.DMA((edge_blocks,))],
        input_output_aliases={3: 0},
        compiler_params=params(12),
        name="settle",
    )(core_arg, edge_table, taken, coupling)
    return basis_out, coupling


def solution(mesh):
    return jax.shard_map(
        body,
        mesh=mesh,
        in_specs=(P("box", None, None), P("box", "col", None), P("box", None)),
        out_specs=(P("box", "col", None), P("box", None, "col", None)),
        check_vma=False,
    )
```
